32 devices in a mesh: dp: 8 (over z, y), mp: 4 (over x, core).
Axes of the slice: x: 2, y: 2, z: 4, core: 2. Of those that a mesh axis runs over, the one named last changes fastest.
Arguments:
- block_input: bfloat16 [16384, 512], P(('dp', 'mp')), may hold values from -6 to 6
- memory: bfloat16 [32, 512, 512], P('dp', 'mp'), may hold values from -6 to 6
- cotangent: bfloat16 [16384, 512], P(('dp', 'mp')), may hold values from -6 to 6
- neighbour_table: bfloat16 [32768, 512], P('dp'), may hold values from -6 to 6
- requests: int32 [256, 256], P(('dp', 'mp')), may hold values from 0 to 4095, as said below
- counts: int32 [256], P(('dp', 'mp')), may hold values from 128 to 256, as said below
- neighbour_slots: int32 [16384, 4], P(('dp', 'mp')), may hold values from 0 to 2047, as said below
- memory_lengths: int32 [32], P('dp'), may hold values from 0 to 512
- document_lengths: int32 [32], P('dp'), may hold values from 1 to 512, as said below
- first_gain: float32 [512], replicated, may hold values from 0.5 to 1.5
- first_bias: float32 [512], replicated, may hold values from -1.75 to 1.75
- query_weight: bfloat16 [512, 512], P(None, 'mp'), may hold values from -0.25 to 0.25
- key_weight: bfloat16 [512, 512], P(None, 'mp'), may hold values from -0.25 to 0.25
- value_weight: bfloat16 [512, 512], P(None, 'mp'), may hold values from -0.25 to 0.25
- position_weight: bfloat16 [512, 512], P(None, 'mp'), may hold values from -0.25 to 0.25
- content_bias: float32 [512], P('mp'), may hold values from -3 to 3
- position_bias: float32 [512], P('mp'), may hold values from -3 to 3
- output_weight: bfloat16 [512, 512], P('mp'), may hold values from -2 to 2
- second_gain: float32 [512], replicated, may hold values from 0.5 to 1.5
- second_bias: float32 [512], replicated, may hold values from -1.75 to 1.75
- inner_weight: bfloat16 [512, 2048], P(None, 'mp'), may hold values from -0.25 to 0.25
- inner_bias: bfloat16 [2048], P('mp'), may hold values from -3 to 3
- outer_weight: bfloat16 [2048, 512], P('mp'), may hold values from -0.125 to 0.125
- outer_bias: float32 [512], replicated, may hold values from -1.75 to 1.75
- gate_weight: float32 [512], replicated, may hold values from -0.25 to 0.25
Outputs:
- mixed_output: bfloat16 [16384, 512], P(('dp', 'mp'))
- input_grad: float32 [16384, 512], P(('dp', 'mp'))
- first_gain_grad: float32 [512], replicated
- first_bias_grad: float32 [512], replicated
- query_weight_grad: float32 [512, 512], P(None, 'mp')
- key_weight_grad: float32 [512, 512], P(None, 'mp')
- value_weight_grad: float32 [512, 512], P(None, 'mp')
- position_weight_grad: float32 [512, 512], P(None, 'mp')
- content_bias_grad: float32 [512], P('mp')
- position_bias_grad: float32 [512], P('mp')
- output_weight_grad: float32 [512, 512], P('mp')
- second_gain_grad: float32 [512], replicated
- second_bias_grad: float32 [512], replicated
- inner_weight_grad: float32 [512, 2048], P(None, 'mp')
- inner_bias_grad: float32 [2048], P('mp')
- outer_weight_grad: float32 [2048, 512], P('mp')
- outer_bias_grad: float32 [512], replicated
- gate_weight_grad: float32 [512], replicated
The draws below stay inside these ranges and needn't reach their ends.
Inputs may be any that keep to these rules, and one draw needn't show every extreme that they name: `neighbour_slots`: each entry is 256 * o + p for an owner o and a place p below the count of that owner's list on the token's device. `requests`: row numbers within the owner's shard of neighbour_table; entries at or past a list's count are filler. `counts`: every device has a list filled to 256, and one owner receives 256 entries from every device. `document_lengths`: in each index of dp one row is 512 long.
All inputs are finite; a program needn't handle non-finite values.
Results may differ from the reference program's by a relative error of at most 0.015.
Values may be sent and summed in bfloat16 or wider, within the bound.
No kernel may reach another device: no remote copies, remote signals or barrier semaphores. Data moves between devices by JAX's collectives and lax.ppermute only.
A program may use at most 192 MiB of HBM per device.

```python
import math
import jax
import jax.numpy as jnp
from jax import lax

D = 512
HEADS = 8
HD = 64
FF = 2048
NBR = 4
SEG = 512
MEM = 512
ROWS_DP = 4
TAB_DEV = 4096
KEYS = 1024
TOK_LOCAL = 512
TOKENS = 16384
ROWS_ALL = 32
CAP = 256
LISTS = 256
N_DP = 8
N_MP = 4


def shared_counts(key):
    first_key, second_key, third_key = jax.random.split(jax.random.fold_in(key, 17), 3)
    sources = N_DP * N_MP
    drawn_counts = jax.random.randint(first_key, (sources, N_DP), CAP // 2, CAP + 1)
    own_full = jax.random.randint(second_key, (sources, 1), 0, N_DP)
    common_full = jax.random.randint(third_key, (1, 1), 0, N_DP)
    column = jnp.arange(N_DP, dtype=jnp.int32)[None, :]
    return jnp.where((column == own_full) | (column == common_full), CAP, drawn_counts).astype(jnp.int32)


def draw_counts(key, part):
    counts_table = shared_counts(key)
    return counts_table.reshape(-1)


def draw_neighbour_slots(key, part):
    counts_table = shared_counts(key)
    key = jax.random.fold_in(key, 2)
    owner_key, place_key = jax.random.split(key)
    owner_dev = jax.random.randint(owner_key, (TOKENS, NBR), 0, N_DP)
    source_dev = jnp.arange(TOKENS, dtype=jnp.int32) // TOK_LOCAL
    limits = counts_table[source_dev[:, None], owner_dev]
    place_in = jax.random.randint(place_key, (TOKENS, NBR), 0, limits)
    return (owner_dev * CAP + place_in).astype(jnp.int32)


def draw_requests(key, part):
    key = jax.random.fold_in(key, 3)
    return jax.random.randint(key, (LISTS, CAP), 0, TAB_DEV).astype(jnp.int32)


def draw_document_lengths(key, part):
    key = jax.random.fold_in(key, 4)
    length_key, pick_key = jax.random.split(key)
    lengths = jax.random.randint(length_key, (ROWS_ALL,), 1, SEG + 1)
    picked = jax.random.randint(pick_key, (N_DP,), 0, ROWS_DP)
    row_number = jnp.arange(ROWS_ALL, dtype=jnp.int32)
    full_row = row_number % ROWS_DP == picked[row_number // ROWS_DP]
    return jnp.where(full_row, SEG, lengths).astype(jnp.int32)


def with_ends(drawn, key, low, largest):
    place = [jax.random.randint(jax.random.fold_in(key, axis), (), 0, length) for axis, length in enumerate(drawn.shape)]
    longest = drawn.shape.index(max(drawn.shape))
    neighbour = place[:longest] + [(place[longest] + 1) % drawn.shape[longest]] + place[longest + 1:]
    return drawn.at[tuple(place)].set(low).at[tuple(neighbour)].set(largest)


def steps_of(own_key, shape, cuts, smallest, top_value):
    loudness, own = 1.0, jax.random.fold_in(own_key, 6)
    for dim, parts in cuts:
        heights = jnp.exp(jax.random.uniform(jax.random.fold_in(own, dim), (parts,), jnp.float32, smallest / len(cuts), top_value / len(cuts)))
        loudness = loudness * jnp.repeat(heights, shape[dim] // parts).reshape([-1 if axis == dim else 1 for axis in range(len(shape))])
    return loudness


def gaussian(rng, dims, scale, most, shards=(), held_as=jnp.bfloat16):
    loudness = steps_of(rng, dims, shards, -0.22, 0.18) if shards else 1.0
    values = jax.random.normal(rng, dims, jnp.float32) * scale * loudness
    return jnp.minimum(jnp.maximum(values, -most), most).astype(held_as)


def setup_inputs(seed: int = 0) -> dict:
    splits = jax.random.split(jax.random.key(seed), 26)
    block_input = gaussian(splits[0], (TOKENS, D), 1.0, 6.0, ((0, 32),))
    memory = gaussian(splits[1], (ROWS_ALL, MEM, D), 1.0, 6.0, ((0, 8), (1, 4)))
    cotangent = gaussian(splits[2], (TOKENS, D), 1.0, 6.0, ((0, 32),))
    neighbour_table = gaussian(splits[3], (N_DP * TAB_DEV, D), 1.0, 6.0, ((0, 8),))
    requests = draw_requests(jax.random.fold_in(splits[25], 71), 0)
    counts = draw_counts(jax.random.fold_in(splits[25], 71), 0)
    neighbour_slots = draw_neighbour_slots(jax.random.fold_in(splits[25], 71), 0)
    memory_lengths = with_ends(jax.random.randint(splits[7], (ROWS_ALL,), 0, MEM + 1), jax.random.fold_in(splits[7], 1), 0, MEM).astype(jnp.int32)
    document_lengths = draw_document_lengths(jax.random.fold_in(splits[25], 71), 0)
    first_gain = jnp.clip(1.0 + 0.1 * jax.random.normal(splits[9], (D,), jnp.float32), 0.5, 1.5)
    first_bias = gaussian(splits[10], (D,), 0.3, 1.75, (), jnp.float32)
    query_weight = gaussian(splits[11], (D, D), D ** -0.5, 0.25, ((1, 4),))
    key_weight = gaussian(splits[12], (D, D), D ** -0.5, 0.25, ((1, 4),))
    value_weight = gaussian(splits[13], (D, D), D ** -0.5, 0.25, ((1, 4),))
    position_weight = gaussian(splits[14], (D, D), D ** -0.5, 0.25, ((1, 4),))
    content_bias = gaussian(splits[15], (D,), 0.5, 3.0, ((0, 4),), jnp.float32)
    position_bias = gaussian(splits[16], (D,), 0.5, 3.0, ((0, 4),), jnp.float32)
    output_weight = gaussian(splits[17], (D, D), (D // 64) ** -0.5, 2.0, ((0, 4),))
    second_gain = jnp.clip(1.0 + 0.1 * jax.random.normal(splits[18], (D,), jnp.float32), 0.5, 1.5)
    second_bias = gaussian(splits[19], (D,), 0.3, 1.75, (), jnp.float32)
    inner_weight = gaussian(splits[20], (D, FF), D ** -0.5, 0.25, ((1, 4),))
    inner_bias = gaussian(splits[21], (FF,), 0.5, 3.0, ((0, 4),))
    outer_weight = gaussian(splits[22], (FF, D), FF ** -0.5, 0.125, ((0, 4),))
    outer_bias = gaussian(splits[23], (D,), 0.3, 1.75, (), jnp.float32)
    gate_weight = gaussian(splits[24], (D,), D ** -0.5, 0.25, (), jnp.float32)
    return dict(block_input=block_input, memory=memory, cotangent=cotangent, neighbour_table=neighbour_table, requests=requests, counts=counts, neighbour_slots=neighbour_slots, memory_lengths=memory_lengths, document_lengths=document_lengths, first_gain=first_gain, first_bias=first_bias, query_weight=query_weight, key_weight=key_weight, value_weight=value_weight, position_weight=position_weight, content_bias=content_bias, position_bias=position_bias, output_weight=output_weight, second_gain=second_gain, second_bias=second_bias, inner_weight=inner_weight, inner_bias=inner_bias, outer_weight=outer_weight, outer_bias=outer_bias, gate_weight=gate_weight)


epsilon = 1e-05
highest = lax.Precision.HIGHEST

@jax.custom_vjp
def low(v):
    return lax.optimization_barrier(v.astype(jnp.bfloat16)).astype(jnp.float32)

@jax.custom_vjp
def low_back(v):
    return v

def low_keep(v):
    return (low(v), None)

def low_pass(kept, grad):
    return (grad,)

def back_keep(v):
    return (v, None)

def back_low(kept, grad):
    return (low(grad),)
low.defvjp(low_keep, low_pass)
low_back.defvjp(back_keep, back_low)

def norm_rows(values, gains, offsets):
    average = lax.optimization_barrier(jnp.mean(values, axis=-1, keepdims=True))
    centred = values - average
    spread = lax.optimization_barrier(jnp.mean(centred * centred, axis=-1, keepdims=True))
    return centred * lax.rsqrt(spread + epsilon) * gains + offsets

def position_table():
    distance = (KEYS - 1 - jnp.arange(KEYS, dtype=jnp.int32)).astype(jnp.float32)
    exponent = jnp.arange(0, D, 2, dtype=jnp.int32).astype(jnp.float32) / D
    angles = distance[:, None] * jnp.exp(-math.log(10000.0) * exponent)[None, :]
    return jnp.concatenate([jnp.sin(angles), jnp.cos(angles)], axis=1)

def shift_rows(scores):
    leading = scores.shape[:-2]
    padding = [(0, 0)] * len(leading) + [(0, 0), (1, 0)]
    padded = jnp.pad(scores, padding)
    folded = padded.reshape(leading + (KEYS + 1, SEG))[..., 1:, :]
    return folded.reshape(leading + (SEG, KEYS))

def row_mask(memory_count, document_count):
    key_place = lax.broadcasted_iota(jnp.int32, (SEG, KEYS), 1)
    query_place = lax.broadcasted_iota(jnp.int32, (SEG, KEYS), 0)
    return (key_place >= MEM - memory_count) & (key_place <= MEM + query_place) & (key_place < MEM + document_count)

def mixing(hidden_state, nearby, gate_proj):
    relevance = jnp.einsum('td,tkd->tk', hidden_state, nearby, precision=highest) / math.sqrt(hidden_state.shape[-1])
    attention = jax.nn.softmax(relevance, axis=-1)
    recalled = jnp.einsum('tk,tkd->td', attention, nearby, precision=highest)
    gating = jax.nn.sigmoid(jnp.dot(hidden_state, gate_proj, precision=highest))
    return hidden_state + gating[:, None] * (recalled - hidden_state)

def reference(block_input, memory, cotangent, neighbour_table, requests, counts, neighbour_slots, memory_lengths, document_lengths, first_gain, first_bias, query_weight, key_weight, value_weight, position_weight, content_bias, position_bias, output_weight, second_gain, second_bias, inner_weight, inner_bias, outer_weight, outer_bias, gate_weight):
    rows_all = ROWS_DP * N_DP
    source_dev = jnp.arange(TOKENS, dtype=jnp.int32) // TOK_LOCAL
    owner_dev = neighbour_slots // CAP
    place_in = neighbour_slots % CAP
    list_row = source_dev[:, None] * N_DP + owner_dev
    table_rows = (owner_dev * TAB_DEV + requests[list_row, place_in]).reshape(rows_all, SEG, NBR)
    live_mask = (place_in < counts[list_row]).astype(jnp.float32).reshape(rows_all, SEG, NBR)
    valid_mask = (jnp.arange(SEG, dtype=jnp.int32)[None, :] < document_lengths[:, None]).astype(jnp.float32)
    grad_mixed = cotangent.astype(jnp.float32).reshape(rows_all, SEG, D) * valid_mask[:, :, None]
    memory_rows = memory.astype(jnp.float32)
    position_low = low(position_table())
    score_scale = HD ** (-0.5)

    def forward(inputs, gains_one, offsets_one, query_proj, key_proj, value_proj, position_proj, bias_content, bias_position, out_proj, gains_two, offsets_two, inner_proj, bias_inner, outer_proj, bias_outer, gate_proj):
        position_keys = low(jnp.dot(position_low, position_proj, precision=highest)).reshape(KEYS, HEADS, HD)

        def one_row(row_items):
            row_input, row_memory, memory_count, document_count, row_tables, row_live = row_items
            normed = low(norm_rows(row_input, gains_one, offsets_one))
            normed_memory = low(norm_rows(row_memory, gains_one, offsets_one))
            keys_in = jnp.concatenate([normed_memory, normed], axis=0)
            query_rows = low_back(jnp.dot(normed, query_proj, precision=highest))
            key_rows = low_back(low(jnp.dot(keys_in, key_proj, precision=highest))).reshape(KEYS, HEADS, HD)
            value_rows = low_back(low(jnp.dot(keys_in, value_proj, precision=highest))).reshape(KEYS, HEADS, HD)
            content_q = low(query_rows + bias_content).reshape(SEG, HEADS, HD)
            position_q = low(query_rows + bias_position).reshape(SEG, HEADS, HD)
            content = jnp.einsum('qhe,khe->hqk', content_q, key_rows, precision=highest)
            position = shift_rows(jnp.einsum('qhe,khe->hqk', position_q, position_keys, precision=highest))
            scores = low_back((content + position) * score_scale)
            scores = jnp.where(row_mask(memory_count, document_count)[None], scores, -1e+30)
            softmaxed = jax.nn.softmax(scores, axis=-1)
            attended = jnp.einsum('hqk,khe->qhe', low(softmaxed), value_rows, precision=highest).reshape(SEG, D)
            attended = low_back(low(attended))
            middle = row_input + low_back(jnp.dot(attended, out_proj, precision=highest))
            normed_middle = low(norm_rows(middle, gains_two, offsets_two))
            preact = low_back(jnp.dot(normed_middle, inner_proj, precision=highest) + bias_inner)
            activation = low(jax.nn.gelu(preact))
            hidden = middle + low_back(jnp.dot(activation, outer_proj, precision=highest)) + bias_outer
            nearby = neighbour_table[row_tables].astype(jnp.float32) * row_live[:, :, None]
            return mixing(hidden, nearby, gate_proj)
        return lax.map(jax.checkpoint(one_row), (inputs, memory_rows, memory_lengths, document_lengths, table_rows, live_mask))
    params = tuple((array.astype(jnp.float32) for array in (block_input.reshape(rows_all, SEG, D), first_gain, first_bias, query_weight, key_weight, value_weight, position_weight, content_bias, position_bias, output_weight, second_gain, second_bias, inner_weight, inner_bias, outer_weight, outer_bias, gate_weight)))
    mixed, pullback = jax.vjp(forward, *params)
    grads = pullback(grad_mixed)
    return (mixed.reshape(TOKENS, D).astype(jnp.bfloat16), grads[0].reshape(TOKENS, D), grads[1], grads[2], grads[3], grads[4], grads[5], grads[6], grads[7], grads[8], grads[9], grads[10], grads[11], grads[12], grads[13], grads[14], grads[15], grads[16])
```

```python
import math

import jax
import jax.numpy as jnp
import numpy as np
from jax import lax
from jax.experimental import pallas as pl
from jax.experimental.pallas import tpu as pltpu
from jax.sharding import PartitionSpec as P

D = 512
HD = 64
SEG = 512
MEM = 512
KEYS = 1024
SLOT = 128
EPS = 1e-05
F32 = jnp.float32
BF16 = jnp.bfloat16
GELU_C = math.sqrt(2.0 / math.pi)
SCALE = HD ** (-0.5)
VMEM = pl.BlockSpec(memory_space=pltpu.VMEM)
SMEM = pl.BlockSpec(memory_space=pltpu.SMEM)


def position_table():
    distance = (KEYS - 1 - np.arange(KEYS)).astype(np.float32)
    exponent = np.arange(0, D, 2).astype(np.float32) / np.float32(D)
    angles = distance[:, None] * np.exp(np.float32(-math.log(10000.0)) * exponent)[None, :]
    table = np.concatenate([np.sin(angles), np.cos(angles)], axis=1).astype(np.float32)
    return jnp.asarray(table).astype(BF16)


def call(body, outs, ins, flops=0, scratch=(), smem=0, vmem=56):
    nbytes = sum(a.size * a.dtype.itemsize for a in ins)
    return pl.pallas_call(
        body,
        out_shape=outs,
        in_specs=[SMEM] * smem + [VMEM] * (len(ins) - smem),
        out_specs=jax.tree.map(lambda _: VMEM, outs),
        scratch_shapes=list(scratch),
        compiler_params=pltpu.CompilerParams(vmem_limit_bytes=vmem * 2**20),
        cost_estimate=pl.CostEstimate(flops=flops, bytes_accessed=nbytes, transcendentals=0),
    )(*ins)


def shape(dims, dtype):
    return jax.ShapeDtypeStruct(dims, dtype)


def mm(a, b):
    return jnp.dot(a, b, preferred_element_type=F32)


def mm_nt(a, b):
    return lax.dot_general(a, b, (((1,), (1,)), ((), ())), preferred_element_type=F32)


def mm_tn(a, b):
    return lax.dot_general(a, b, (((0,), (0,)), ((), ())), preferred_element_type=F32)


def mm_tt(a, b):
    return lax.dot_general(a, b, (((0,), (1,)), ((), ())), preferred_element_type=F32)


def norm_parts(values):
    average = jnp.mean(values, axis=-1, keepdims=True)
    centred = values - average
    spread = jnp.mean(centred * centred, axis=-1, keepdims=True)
    inverse = lax.rsqrt(spread + EPS)
    return centred * inverse, inverse


def norm_back(grad, gain, xhat, inverse):
    scaled = grad * gain
    return inverse * (
        scaled
        - jnp.mean(scaled, axis=-1, keepdims=True)
        - xhat * jnp.mean(scaled * xhat, axis=-1, keepdims=True)
    )


def head_lanes(rows, h):
    lane = lax.broadcasted_iota(jnp.int32, (rows, SLOT), 1)
    return (lane // HD) == h


def of_head(values, h):
    return jnp.where(head_lanes(values.shape[0], h), values, jnp.zeros_like(values))


def norm_kernel(place_ref, x_ref, m0, m1, m2, m3, g_ref, b_ref, keys_ref):
    me = place_ref[0]
    gain, bias = g_ref[...], b_ref[...]
    for k, block in enumerate((m0, m1, m2, m3)):
        xhat, _ = norm_parts(block[...].astype(F32))
        start = pl.multiple_of((me ^ k) * SLOT, SLOT)
        keys_ref[pl.ds(start, SLOT), :] = (xhat * gain + bias).astype(BF16)
    xhat, _ = norm_parts(x_ref[...].astype(F32))
    keys_ref[MEM:, :] = (xhat * gain + bias).astype(BF16)


def attend_kernel(
    place_ref, mem_ref, doc_ref,
    keys_ref, table_ref, q0, q1, k0, k1, v0, v1, p0, p1, s0, s1,
    probs_ref, qc_ref, qp_ref, kr_ref, vr_ref, pk_ref, att_ref,
    bias_ref,
):
    row = place_ref[0]
    low = MEM - mem_ref[row]
    high = MEM + doc_ref[row]
    place_k = lax.broadcasted_iota(jnp.int32, (SEG, KEYS), 1)
    place_q = lax.broadcasted_iota(jnp.int32, (SEG, KEYS), 0)
    live = (place_k >= low) & (place_k <= MEM + place_q) & (place_k < high)
    bias_ref[...] = jnp.where(live, 0.0, -1e30)
    keys_in = keys_ref[...]
    normed = keys_ref[MEM:, :]
    for s, (wq, wk, wv, wp, small) in enumerate(
        ((q0, k0, v0, p0, s0), (q1, k1, v1, p1, s1))
    ):
        query = mm(normed, wq[...])
        qc_ref[s] = (query + small[1:2, :SLOT]).astype(BF16)
        qp_ref[s] = (query + small[1:2, SLOT : 2 * SLOT]).astype(BF16)
        kr_ref[s] = mm(keys_in, wk[...]).astype(BF16)
        vr_ref[s] = mm(keys_in, wv[...]).astype(BF16)
        pk_ref[s] = mm(table_ref[...], wp[...]).astype(BF16)
    for s in range(2):
        parts = []
        for h in range(2):
            content = mm_nt(of_head(qc_ref[s], h), kr_ref[s])
            place = mm_nt(of_head(qp_ref[s], h), pk_ref[s])
            place = pltpu.roll(place, KEYS - SEG + 1, 1, stride=1, stride_axis=0)
            scores = (content + place) * SCALE + bias_ref[...]
            largest = jnp.max(scores, axis=-1, keepdims=True)
            raised = jnp.exp(scores - largest)
            total = jnp.sum(raised, axis=-1, keepdims=True)
            probs = (raised * (1.0 / total)).astype(BF16)
            probs_ref[2 * s + h] = probs
            parts.append(mm(probs, vr_ref[s]))
        att_ref[s] = jnp.where(head_lanes(SEG, 0), parts[0], parts[1]).astype(BF16)


def feed_kernel(
    x_ref, att_a, att_b, o0, o1, o2, o3, g_ref, b_ref,
    i0, i1, i2, i3, s0, s1, s2, s3, u0, u1, u2, u3, ob_ref,
    middle_ref, hidden_ref, nm_ref, act_ref, slope_ref,
):
    middle = x_ref[...].astype(F32)
    for att, w in ((att_a[0], o0), (att_a[1], o1), (att_b[0], o2), (att_b[1], o3)):
        middle = middle + mm(att, w[...])
    middle_ref[...] = middle
    xhat, _ = norm_parts(middle)
    normed = (xhat * g_ref[...] + b_ref[...]).astype(BF16)
    nm_ref[...] = normed
    hidden = middle + ob_ref[...]
    for s, (wi, small, wo) in enumerate(((i0, s0, u0), (i1, s1, u1), (i2, s2, u2), (i3, s3, u3))):
        pre = mm(normed, wi[...]) + small[0:1, :]
        square = pre * pre
        bend = jnp.tanh(GELU_C * (pre + 0.044715 * (pre * square)))
        act = (0.5 * pre * (1.0 + bend)).astype(BF16)
        slope = 0.5 * (1.0 + bend) + (0.5 * GELU_C) * pre * (1.0 - bend * bend) * (
            1.0 + (3 * 0.044715) * square
        )
        act_ref[s] = act
        slope_ref[s] = slope.astype(BF16)
        hidden = hidden + mm(act, wo[...])
    hidden_ref[...] = hidden


def mix_kernel(blocks, *refs):
    place_ref, doc_ref = refs[:2]
    fetched_refs = refs[2 : 2 + blocks]
    (
        slots_ref, cot_ref, hidden_ref, gate_ref,
        mixed_ref, gh_ref, gate_grad_ref, fetched,
    ) = refs[2 + blocks :]
    rows = fetched_refs[0].shape[0]
    for n, block in enumerate(fetched_refs):
        fetched[n * rows : (n + 1) * rows, :] = block[...]
    total = blocks * rows
    docs = doc_ref[place_ref[0]]
    gate = gate_ref[...]
    scale = 1.0 / math.sqrt(D)
    step = 128
    gate_grad = jnp.zeros((1, D), F32)
    for c in range(SEG // step):
        span = slice(c * step, (c + 1) * step)
        lane = lax.broadcasted_iota(jnp.int32, (step, total), 1)
        near = []
        for j in range(4):
            pick = jnp.where(slots_ref[span, j : j + 1] == lane, 1.0, 0.0).astype(BF16)
            near.append(mm(pick, fetched[...]))
        hidden = hidden_ref[span, :]
        token = c * step + lax.broadcasted_iota(jnp.int32, (step, 1), 0)
        grad_mixed = cot_ref[span, :].astype(F32) * jnp.where(token < docs, 1.0, 0.0)
        rel = [jnp.sum(hidden * n, axis=-1, keepdims=True) * scale for n in near]
        top = jnp.maximum(jnp.maximum(rel[0], rel[1]), jnp.maximum(rel[2], rel[3]))
        raised = [jnp.exp(r - top) for r in rel]
        inverse = 1.0 / (raised[0] + raised[1] + raised[2] + raised[3])
        alpha = [r * inverse for r in raised]
        recalled = sum(a * n for a, n in zip(alpha, near))
        logit = jnp.sum(hidden * gate, axis=-1, keepdims=True)
        gating = 1.0 / (1.0 + jnp.exp(-logit))
        apart = recalled - hidden
        mixed_ref[span, :] = (hidden + gating * apart).astype(BF16)
        grad_recalled = gating * grad_mixed
        grad_gating = jnp.sum(grad_mixed * apart, axis=-1, keepdims=True)
        grad_logit = grad_gating * gating * (1.0 - gating)
        grad_alpha = [jnp.sum(grad_recalled * n, axis=-1, keepdims=True) for n in near]
        weighed = sum(a * g for a, g in zip(alpha, grad_alpha))
        grad_rel = [a * (g - weighed) * scale for a, g in zip(alpha, grad_alpha)]
        grad_hidden = grad_mixed - grad_recalled + grad_logit * gate
        grad_hidden = grad_hidden + sum(g * n for g, n in zip(grad_rel, near))
        gh_ref[span, :] = grad_hidden
        gate_grad = gate_grad + jnp.sum(grad_logit * hidden, axis=0, keepdims=True)
    gate_grad_ref[...] = gate_grad


FEED_ROWS = 2 * D + SLOT + 64


def feed_back_kernel(
    gh_ref, gate_grad_ref, middle_ref, nm_ref, act_ref, slope_ref, g_ref,
    att_a, att_b, o0, o1, o2, o3, i0, i1, i2, i3, u0, u1, u2, u3,
    gm_ref, ga_a, ga_b, pay_ref,
):
    grad_hidden = gh_ref[...]
    low = grad_hidden.astype(BF16)
    low_t = low.T
    normed_t = nm_ref[...].T
    outer_bias_grad = jnp.sum(grad_hidden, axis=0, keepdims=True)
    grad_nm = jnp.zeros((SEG, D), F32)
    bias_rows = []
    for s, (wi, wo) in enumerate(((i0, u0), (i1, u1), (i2, u2), (i3, u3))):
        grad_act = mm_nt(low, wo[...])
        grad_pre = (grad_act * slope_ref[s].astype(F32)).astype(BF16)
        pay_ref[s, D : 2 * D, :] = mm(low_t, act_ref[s]).astype(BF16)
        pay_ref[s, 0:D, :] = mm(normed_t, grad_pre).astype(BF16)
        bias_rows.append(jnp.sum(grad_pre.astype(F32), axis=0, keepdims=True))
        grad_nm = grad_nm + mm_nt(grad_pre, wi[...])
    xhat, inverse = norm_parts(middle_ref[...])
    gain_grad = jnp.sum(grad_nm * xhat, axis=0, keepdims=True)
    bias_grad = jnp.sum(grad_nm, axis=0, keepdims=True)
    grad_middle = grad_hidden + norm_back(grad_nm, g_ref[...], xhat, inverse)
    gm_ref[...] = grad_middle
    middle_low = grad_middle.astype(BF16)
    zeros = jnp.zeros((59, D), F32)
    for s, (att, w) in enumerate(
        ((att_a[0], o0), (att_a[1], o1), (att_b[0], o2), (att_b[1], o3))
    ):
        pay_ref[s, 2 * D : 2 * D + SLOT, :] = mm_tn(att, middle_low).astype(BF16)
        grad_att = mm_nt(middle_low, w[...]).astype(BF16)
        (ga_a if s < 2 else ga_b)[s % 2] = grad_att
        tail = jnp.concatenate(
            [bias_rows[s], gain_grad, bias_grad, outer_bias_grad, gate_grad_ref[...], zeros], axis=0
        )
        pay_ref[s, 2 * D + SLOT :, :] = tail.astype(BF16)


HEAD_ROWS = 4 * SLOT + 64


def attend_back_kernel(
    last,
    *refs,
):
    (
        keys_ref, table_ref, probs_ref, qc_ref, qp_ref, kr_ref, vr_ref, pk_ref, ga_ref,
        q0, q1, k0, k1, v0, v1,
    ) = refs[:15]
    if last:
        dk_in, gm_ref, x_ref, m0, m1, m2, m3, place_ref, g_ref = refs[15:24]
        pay_ref, grad_ref = refs[24:26]
        dk_ref = refs[26]
    else:
        pay_ref, dk_ref = refs[15:17]
    half = SEG // 2
    across = lax.broadcasted_iota(jnp.int32, (half, half), 1)
    down = lax.broadcasted_iota(jnp.int32, (half, half), 0)
    swap = jnp.where(across + down == half - 1, 1.0, 0.0).astype(BF16)

    def flip(values):
        return jnp.concatenate([mm(swap, values[half:]), mm(swap, values[:half])], axis=0)

    keys_in = keys_ref[...]
    normed = keys_ref[MEM:, :]
    for s, (wq, wk, wv) in enumerate(((q0, k0, v0), (q1, k1, v1))):
        grad_v = jnp.zeros((SLOT, KEYS), F32)
        grad_k = jnp.zeros((SLOT, KEYS), F32)
        grad_p = jnp.zeros((SLOT, KEYS), F32)
        grad_c = jnp.zeros((SEG, SLOT), F32)
        grad_place = jnp.zeros((SEG, SLOT), F32)
        qp_flip = flip(qp_ref[s]).astype(BF16)
        for h in range(2):
            probs = probs_ref[2 * s + h]
            grad_out = of_head(ga_ref[s], h)
            grad_probs = mm_nt(grad_out, vr_ref[s])
            wide = probs.astype(F32)
            weighed = jnp.sum(wide * grad_probs, axis=-1, keepdims=True)
            grad_scores = (wide * (grad_probs - weighed)).astype(BF16)
            grad_v = grad_v + mm_tn(grad_out, probs)
            grad_k = grad_k + mm_tn(of_head(qc_ref[s], h), grad_scores)
            grad_c = grad_c + mm(grad_scores, of_head(kr_ref[s], h))
            turned = pltpu.roll(flip(grad_scores), 0, 1, stride=1, stride_axis=0).astype(BF16)
            grad_place = grad_place + mm(turned, of_head(pk_ref[s], h))
            grad_p = grad_p + mm_tn(of_head(qp_flip, h), turned)
        grad_v = grad_v.astype(BF16)
        grad_k = (grad_k * SCALE).astype(BF16)
        grad_p = (grad_p * SCALE).astype(BF16)
        grad_c = grad_c * SCALE
        grad_place = grad_place * SCALE
        high = grad_place.astype(BF16)
        rest = (grad_place - high.astype(F32)).astype(BF16)
        grad_q = (grad_c + flip(high) + flip(rest)).astype(BF16)
        pay_ref[s, 0:SLOT, :] = mm_tn(grad_q, normed).astype(BF16)
        pay_ref[s, SLOT : 2 * SLOT, :] = mm(grad_k, keys_in).astype(BF16)
        pay_ref[s, 2 * SLOT : 3 * SLOT, :] = mm(grad_v, keys_in).astype(BF16)
        pay_ref[s, 3 * SLOT : 4 * SLOT, :] = mm(grad_p, table_ref[...]).astype(BF16)
        biases = jnp.concatenate(
            [
                jnp.sum(grad_c, axis=0, keepdims=True),
                jnp.sum(grad_place, axis=0, keepdims=True),
                jnp.zeros((1, D - 2 * SLOT), F32),
            ],
            axis=1,
        )
        pay_ref[s, 4 * SLOT :, :] = jnp.concatenate(
            [biases, jnp.zeros((63, D), F32)], axis=0
        ).astype(BF16)
        both = jnp.concatenate([grad_k, grad_v], axis=0)
        weights = jnp.concatenate([wk[...], wv[...]], axis=1)
        grad_keys = mm_tt(both, weights)
        grad_rows = mm_nt(grad_q, wq[...])
        if s == 0 and not last:
            dk_ref[:MEM, :] = grad_keys[:MEM]
            dk_ref[MEM:, :] = grad_keys[MEM:] + grad_rows
        else:
            before = dk_in if (s == 0) else dk_ref
            dk_ref[:MEM, :] = before[:MEM, :] + grad_keys[:MEM]
            dk_ref[MEM:, :] = before[MEM:, :] + grad_keys[MEM:] + grad_rows
    if last:
        gain = g_ref[...]
        me = place_ref[0]
        xhat, inverse = norm_parts(x_ref[...].astype(F32))
        grad = dk_ref[MEM:, :]
        grad_ref[...] = gm_ref[...] + norm_back(grad, gain, xhat, inverse)
        gain_grad = jnp.sum(grad * xhat, axis=0, keepdims=True)
        bias_grad = jnp.sum(dk_ref[...], axis=0, keepdims=True)
        for k, block in enumerate((m0, m1, m2, m3)):
            xhat, _ = norm_parts(block[...].astype(F32))
            start = pl.multiple_of((me ^ k) * SLOT, SLOT)
            gain_grad = gain_grad + jnp.sum(
                dk_ref[pl.ds(start, SLOT), :] * xhat, axis=0, keepdims=True
            )
        tail = jnp.concatenate([gain_grad, bias_grad], axis=0)
        for s in range(2):
            pay_ref[s, 4 * SLOT + 8 : 4 * SLOT + 16, :] = jnp.concatenate(
                [tail, jnp.zeros((6, D), F32)], axis=0
            ).astype(BF16)


def swap_with(values, axis, k):
    n = lax.axis_size(axis)
    return lax.ppermute(values, axis, [(i, i ^ k) for i in range(n)])


def add_low(*terms):
    return sum(t.astype(F32) for t in terms).astype(BF16)


def sum_over(values, axis):
    n = lax.axis_size(axis)
    me = lax.axis_index(axis)
    steps = []
    k = 1
    while k < min(n, 8) and values.shape[0] % 16 == 0:
        half = values.shape[0] // 2
        bit = (me // k) % 2
        sent = lax.dynamic_slice_in_dim(values, (1 - bit) * half, half)
        kept = lax.dynamic_slice_in_dim(values, bit * half, half)
        values = add_low(kept, swap_with(sent, axis, k))
        steps.append((k, bit))
        k *= 2
    while k < n:
        values = add_low(values, swap_with(values, axis, k))
        k *= 2
    for k, bit in reversed(steps):
        other = swap_with(values, axis, k)
        first = jnp.where(bit == 0, values, other)
        second = jnp.where(bit == 0, other, values)
        values = jnp.concatenate([first, second], axis=0)
    return values


def all_shards(values):
    one = swap_with(values, "mp", 1)
    two = swap_with(values, "mp", 2)
    three = swap_with(two, "mp", 1)
    return [values, one, two, three]


def local(
    block_input,
    memory,
    cotangent,
    neighbour_table,
    requests,
    counts,
    neighbour_slots,
    memory_lengths,
    document_lengths,
    first_gain,
    first_bias,
    query_weight,
    key_weight,
    value_weight,
    position_weight,
    content_bias,
    position_bias,
    output_weight,
    second_gain,
    second_bias,
    inner_weight,
    inner_bias,
    outer_weight,
    outer_bias,
    gate_weight,
):
    model_index = lax.axis_index("mp").astype(jnp.int32)
    data_index = lax.axis_index("dp").astype(jnp.int32)
    data_size = lax.axis_size("dp")
    place = model_index.reshape(1)
    capacity = requests.shape[1]
    row = lambda v: v.reshape(1, -1)
    g1, b1, g2, b2 = row(first_gain), row(first_bias), row(second_gain), row(second_bias)

    def memory_of(k):
        return lax.dynamic_index_in_dim(memory, model_index ^ k, 0, keepdims=False)

    mem_blocks = [memory_of(0)] + [swap_with(memory_of(k), "mp", k) for k in (1, 2, 3)]

    if data_size <= 8:
        wanted = [lax.dynamic_index_in_dim(requests, data_index, 0, keepdims=False)]
        for k in range(1, data_size):
            mine = lax.dynamic_index_in_dim(requests, data_index ^ k, 0, keepdims=True)
            wanted.append(swap_with(mine, "dp", k)[0])
        found = jnp.take(neighbour_table, jnp.stack(wanted), axis=0, mode="clip")
        fetched = [found[0]] + [swap_with(found[k], "dp", k) for k in range(1, data_size)]
        slots = neighbour_slots ^ (data_index * capacity)
    else:
        wanted = lax.all_to_all(requests, "dp", split_axis=0, concat_axis=0, tiled=True)
        found = jnp.take(neighbour_table, wanted, axis=0, mode="clip")
        back = lax.all_to_all(found, "dp", split_axis=0, concat_axis=0, tiled=True)
        fetched = [back.reshape(data_size * capacity, D)]
        slots = neighbour_slots

    small = jnp.concatenate(
        [
            row(inner_bias.astype(F32)),
            jnp.concatenate([row(content_bias), row(position_bias)] * 2, axis=1),
        ],
        axis=0,
    )
    smalls = all_shards(small)
    wq, wk, wv, wp = (
        all_shards(w) for w in (query_weight, key_weight, value_weight, position_weight)
    )
    wo = all_shards(output_weight)
    wi = all_shards(inner_weight)
    wu = all_shards(outer_weight)
    table = position_table()

    (keys_in,) = call(
        norm_kernel, (shape((KEYS, D), BF16),), [place, block_input, *mem_blocks, g1, b1], smem=1
    )

    def attend(a, b):
        slot = lambda rows: shape((2, rows, SLOT), BF16)
        ins = [place, memory_lengths, document_lengths, keys_in, table]
        for w in (wq, wk, wv, wp, smalls):
            ins += [w[a], w[b]]
        return call(
            attend_kernel,
            (
                shape((4, SEG, KEYS), BF16),
                slot(SEG), slot(SEG), slot(KEYS), slot(KEYS), slot(KEYS), slot(SEG),
            ),
            ins,
            flops=2 * 10**10,
            scratch=[pltpu.VMEM((SEG, KEYS), F32)],
            smem=3,
        )

    saved_a = attend(0, 1)
    saved_b = attend(2, 3)
    att_a, att_b = saved_a[-1], saved_b[-1]

    square = shape((SEG, D), F32)
    middle, hidden, normed_middle, activation, slope = call(
        feed_kernel,
        (
            square, square, shape((SEG, D), BF16),
            shape((4, SEG, D), BF16), shape((4, SEG, D), BF16),
        ),
        [block_input, att_a, att_b, *wo, g2, b2, *wi, *smalls, *wu, row(outer_bias)],
        flops=6 * 10**9,
    )

    def mix_body(*refs):
        mix_kernel(len(fetched), *refs)

    mixed, grad_hidden, grad_gate = call(
        mix_body,
        (shape((SEG, D), BF16), square, shape((1, D), F32)),
        [place, document_lengths, *fetched, slots, cotangent, hidden, row(gate_weight)],
        flops=6 * 10**9,
        scratch=[pltpu.VMEM((capacity * requests.shape[0], D), BF16)],
        smem=2,
    )
    slot_grad = shape((2, SEG, SLOT), BF16)
    grad_middle, ga_a, ga_b, feed_pay = call(
        feed_back_kernel,
        (square, slot_grad, slot_grad, shape((4, FEED_ROWS, D), BF16)),
        [
            grad_hidden, grad_gate, middle, normed_middle, activation, slope, g2,
            att_a, att_b, *wo, *wi, *wu,
        ],
        flops=10**10,
    )

    pay_shape = shape((2, HEAD_ROWS, D), BF16)

    def back_far(*refs):
        attend_back_kernel(False, *refs)

    def back_near(*refs):
        attend_back_kernel(True, *refs)

    pay_far, grad_keys = call(
        back_far,
        (pay_shape, shape((KEYS, D), F32)),
        [
            keys_in, table, *saved_b[:-1], ga_b,
            wq[2], wq[3], wk[2], wk[3], wv[2], wv[3],
        ],
        flops=2 * 10**10,
    )
    ins = [
        keys_in, table, *saved_a[:-1], ga_a, wq[0], wq[1], wk[0], wk[1], wv[0], wv[1],
        grad_keys, grad_middle, block_input, *mem_blocks, place, g1,
    ]
    specs = [VMEM] * len(ins)
    specs[-2] = SMEM
    pay_near, input_grad = pl.pallas_call(
        back_near,
        out_shape=(pay_shape, square),
        in_specs=specs,
        out_specs=(VMEM, VMEM),
        scratch_shapes=[pltpu.VMEM((KEYS, D), F32)],
        compiler_params=pltpu.CompilerParams(vmem_limit_bytes=56 * 2**20),
        cost_estimate=pl.CostEstimate(flops=2 * 10**10, bytes_accessed=10**7, transcendentals=0),
    )(*ins)

    def to_owner(own, one, two, three):
        far = add_low(two, swap_with(three, "mp", 1))
        near = add_low(own, swap_with(one, "mp", 1))
        return add_low(near, swap_with(far, "mp", 2))

    feed_sum = sum_over(to_owner(*(feed_pay[k] for k in range(4))), "dp")
    tail = 4 * SLOT + 8
    far_0 = jnp.concatenate([pay_far[0, :tail], pay_near[0, tail:]], axis=0)
    far_1 = jnp.concatenate([pay_far[1, :tail], pay_near[1, tail:]], axis=0)
    head_sum = sum_over(to_owner(pay_near[0], pay_near[1], far_0, far_1), "dp")

    wide = head_sum.astype(F32)
    feed = feed_sum.astype(F32)
    vectors = feed[2 * D + SLOT :]
    return (
        mixed,
        input_grad,
        wide[tail],
        wide[tail + 1],
        wide[0:SLOT].T,
        wide[SLOT : 2 * SLOT].T,
        wide[2 * SLOT : 3 * SLOT].T,
        wide[3 * SLOT : 4 * SLOT].T,
        wide[4 * SLOT, :SLOT],
        wide[4 * SLOT, SLOT : 2 * SLOT],
        feed[2 * D : 2 * D + SLOT],
        vectors[1],
        vectors[2],
        feed[0:D],
        vectors[0],
        feed[D : 2 * D].T,
        vectors[3],
        vectors[4],
    )


def solution(mesh):
    return jax.shard_map(
        local,
        mesh=mesh,
        in_specs=(
            P(("dp", "mp"), None),
            P("dp", "mp", None),
            P(("dp", "mp"), None),
            P("dp", None),
            P(("dp", "mp"), None),
            P(("dp", "mp")),
            P(("dp", "mp"), None),
            P("dp"),
            P("dp"),
            P(),
            P(),
            P(None, "mp"),
            P(None, "mp"),
            P(None, "mp"),
            P(None, "mp"),
            P("mp"),
            P("mp"),
            P("mp", None),
            P(),
            P(),
            P(None, "mp"),
            P("mp"),
            P("mp", None),
            P(),
            P(),
        ),
        out_specs=(
            P(("dp", "mp"), None),
            P(("dp", "mp"), None),
            P(),
            P(),
            P(None, "mp"),
            P(None, "mp"),
            P(None, "mp"),
            P(None, "mp"),
            P("mp"),
            P("mp"),
            P("mp", None),
            P(),
            P(),
            P(None, "mp"),
            P("mp"),
            P("mp", None),
            P(),
            P(),
        ),
        check_vma=False,
    )
```

```python
import math

import jax
import jax.numpy as jnp
import numpy as np
from jax import lax
from jax.experimental import pallas as pl
from jax.experimental.pallas import tpu as pltpu
from jax.sharding import PartitionSpec as P

D = 512
HD = 64
SEG = 512
MEM = 512
KEYS = 1024
SLOT = 128
EPS = 1e-05
F32 = jnp.float32
BF16 = jnp.bfloat16
GELU_C = math.sqrt(2.0 / math.pi)
SCALE = HD ** (-0.5)
VMEM = pl.BlockSpec(memory_space=pltpu.VMEM)
SMEM = pl.BlockSpec(memory_space=pltpu.SMEM)
ANY = pl.BlockSpec(memory_space=pl.ANY)


def position_table():
    distance = (KEYS - 1 - np.arange(KEYS)).astype(np.float32)
    exponent = np.arange(0, D, 2).astype(np.float32) / np.float32(D)
    angles = distance[:, None] * np.exp(np.float32(-math.log(10000.0)) * exponent)[None, :]
    table = np.concatenate([np.sin(angles), np.cos(angles)], axis=1).astype(np.float32)
    return jnp.asarray(table).astype(BF16)


def call(body, outs, ins, us=1, scratch=(), smem=0, after=(), vmem=56):
    count = len(ins)

    def run(*refs):
        body(*refs[:count], *refs[count + len(after) :])

    nbytes = sum(a.size * a.dtype.itemsize for a in ins)
    return pl.pallas_call(
        run,
        out_shape=outs,
        in_specs=[SMEM] * smem + [VMEM] * (count - smem) + [ANY] * len(after),
        out_specs=jax.tree.map(lambda _: VMEM, outs),
        scratch_shapes=list(scratch),
        compiler_params=pltpu.CompilerParams(vmem_limit_bytes=vmem * 2**20),
        cost_estimate=pl.CostEstimate(flops=us * 10**9, bytes_accessed=nbytes, transcendentals=0),
    )(*ins, *after)


def shape(dims, dtype):
    return jax.ShapeDtypeStruct(dims, dtype)


def mm(a, b):
    return jnp.dot(a, b, preferred_element_type=F32)


def mm_nt(a, b):
    return lax.dot_general(a, b, (((1,), (1,)), ((), ())), preferred_element_type=F32)


def mm_tn(a, b):
    return lax.dot_general(a, b, (((0,), (0,)), ((), ())), preferred_element_type=F32)


def mm_tt(a, b):
    return lax.dot_general(a, b, (((0,), (1,)), ((), ())), preferred_element_type=F32)


def norm_parts(values):
    average = jnp.mean(values, axis=-1, keepdims=True)
    centred = values - average
    spread = jnp.mean(centred * centred, axis=-1, keepdims=True)
    inverse = lax.rsqrt(spread + EPS)
    return centred * inverse, inverse


def norm_back(grad, gain, xhat, inverse):
    scaled = grad * gain
    return inverse * (
        scaled
        - jnp.mean(scaled, axis=-1, keepdims=True)
        - xhat * jnp.mean(scaled * xhat, axis=-1, keepdims=True)
    )


def head_lanes(rows, h):
    lane = lax.broadcasted_iota(jnp.int32, (rows, SLOT), 1)
    return (lane // HD) == h


def of_head(values, h):
    return jnp.where(head_lanes(values.shape[0], h), values, jnp.zeros_like(values))


HEAD_PACK = D + 16
FEED_PACK = 2 * D + SLOT


def query_of(pack):
    return pack[0:D, 0:SLOT]


def key_value_of(pack):
    return pack[0:D, SLOT : 3 * SLOT]


def place_of(pack):
    return pack[0:D, 3 * SLOT : 4 * SLOT]


def start_kernel(
    place_ref, mem_ref, wq, wk, wv, wp, ib_ref, cb_ref, pb_ref,
    m0, m1, m2, m3, pack_ref,
):
    me = place_ref[0]
    for k, block in enumerate((m0, m1, m2, m3)):
        block[...] = mem_ref[me ^ k]
    for n, w in enumerate((wq, wk, wv, wp)):
        pack_ref[0:D, n * SLOT : (n + 1) * SLOT] = w[...]
    biases = jnp.concatenate([cb_ref[...], pb_ref[...]] * 2, axis=1)
    high = biases.astype(BF16).astype(F32)
    middle = (biases - high).astype(BF16).astype(F32)
    rows = jnp.concatenate(
        [ib_ref[...].astype(F32), high, middle, biases - high - middle, jnp.zeros((12, D), F32)],
        axis=0,
    )
    pack_ref[D:, :] = rows.astype(BF16)


def feed_pack_kernel(wi, wu, wo, pack_ref):
    pack_ref[0:D, :] = wi[...]
    pack_ref[D : 2 * D, :] = wu[...]
    pack_ref[2 * D :, :] = wo[...]


def memory_kernel(place_ref, m0, m1, m2, m3, x_ref, g_ref, b_ref, keys_ref):
    me = place_ref[0]
    for k, block in enumerate((m0, m1, m2, m3)):
        xhat, _ = norm_parts(block[...].astype(F32))
        start = pl.multiple_of((me ^ k) * SLOT, SLOT)
        keys_ref[pl.ds(start, SLOT), :] = (xhat * g_ref[...] + b_ref[...]).astype(BF16)
    xhat, _ = norm_parts(x_ref[...].astype(F32))
    keys_ref[MEM:, :] = (xhat * g_ref[...] + b_ref[...]).astype(BF16)


def attend_kernel(
    place_ref, mem_ref, doc_ref, keys_ref, table_ref, pack,
    probs_ref, qc_ref, qp_ref, kr_ref, vr_ref, pk_ref, att_ref,
    bias_ref,
):
    row = place_ref[0]
    low = MEM - mem_ref[row]
    high = MEM + doc_ref[row]
    place_k = lax.broadcasted_iota(jnp.int32, (SEG, KEYS), 1)
    place_q = lax.broadcasted_iota(jnp.int32, (SEG, KEYS), 0)
    live = (place_k >= low) & (place_k <= MEM + place_q) & (place_k < high)
    bias_ref[...] = jnp.where(live, 0.0, -1e30)
    small = pack[D:, :].astype(F32)
    offsets = small[1:2] + small[2:3] + small[3:4]
    query = mm(keys_ref[MEM:, :], query_of(pack))
    qc_ref[...] = (query + offsets[:, :SLOT]).astype(BF16)
    qp_ref[...] = (query + offsets[:, SLOT : 2 * SLOT]).astype(BF16)
    both = mm(keys_ref[...], key_value_of(pack)).astype(BF16)
    kr_ref[...] = both[:, :SLOT]
    vr_ref[...] = both[:, SLOT:]
    pk_ref[...] = mm(table_ref[...], place_of(pack)).astype(BF16)
    parts = []
    for h in range(2):
        content = mm_nt(of_head(qc_ref[...], h), kr_ref[...])
        place = mm_nt(of_head(qp_ref[...], h), pk_ref[...])
        place = pltpu.roll(place, KEYS - SEG + 1, 1, stride=1, stride_axis=0)
        scores = (content + place) * SCALE + bias_ref[...]
        largest = jnp.max(scores, axis=-1, keepdims=True)
        raised = jnp.exp(scores - largest)
        total = jnp.sum(raised, axis=-1, keepdims=True)
        probs = (raised * (1.0 / total)).astype(BF16)
        probs_ref[h] = probs
        parts.append(mm(probs, vr_ref[...]))
    att_ref[...] = jnp.where(head_lanes(SEG, 0), parts[0], parts[1]).astype(BF16)


def feed_kernel(
    x_ref, t0, t1, t2, t3, g_ref, b_ref, h0, h1, h2, h3, f0, f1, f2, f3, ob_ref,
    middle_ref, hidden_ref, nm_ref, act_ref, slope_ref,
):
    middle = x_ref[...].astype(F32)
    packs = (f0, f1, f2, f3)
    for att, pack in zip((t0, t1, t2, t3), packs):
        middle = middle + mm(att[...], pack[2 * D :, :])
    middle_ref[...] = middle
    xhat, _ = norm_parts(middle)
    normed = (xhat * g_ref[...] + b_ref[...]).astype(BF16)
    nm_ref[...] = normed
    hidden = middle + ob_ref[...]
    for s, (small, pack) in enumerate(zip((h0, h1, h2, h3), packs)):
        pre = mm(normed, pack[0:D, :]) + small[D:, :].astype(F32)[0:1]
        square = pre * pre
        bend = jnp.tanh(GELU_C * (pre + 0.044715 * (pre * square)))
        act = (0.5 * pre * (1.0 + bend)).astype(BF16)
        slope = 0.5 * (1.0 + bend) + (0.5 * GELU_C) * pre * (1.0 - bend * bend) * (
            1.0 + (3 * 0.044715) * square
        )
        act_ref[s] = act
        slope_ref[s] = slope.astype(BF16)
        hidden = hidden + mm(act, pack[D : 2 * D, :])
    hidden_ref[...] = hidden


def mix_kernel(
    place_ref, doc_ref, fetched, slots_ref, cot_ref, hidden_ref, gate_ref,
    act_ref, slope_ref, f0, f1, f2, f3,
    mixed_ref, gh_ref, gate_grad_ref, keep_ref, send_ref, pre_ref,
):
    total = fetched.shape[0]
    docs = doc_ref[place_ref[0]]
    gate = gate_ref[...]
    scale = 1.0 / math.sqrt(D)
    step = 128
    gate_grad = jnp.zeros((1, D), F32)
    for c in range(SEG // step):
        span = slice(c * step, (c + 1) * step)
        lane = lax.broadcasted_iota(jnp.int32, (step, total), 1)
        near = []
        for j in range(4):
            pick = jnp.where(slots_ref[span, j : j + 1] == lane, 1.0, 0.0).astype(BF16)
            near.append(mm(pick, fetched[...]))
        hidden = hidden_ref[span, :]
        token = c * step + lax.broadcasted_iota(jnp.int32, (step, 1), 0)
        grad_mixed = cot_ref[span, :].astype(F32) * jnp.where(token < docs, 1.0, 0.0)
        rel = [jnp.sum(hidden * n, axis=-1, keepdims=True) * scale for n in near]
        top = jnp.maximum(jnp.maximum(rel[0], rel[1]), jnp.maximum(rel[2], rel[3]))
        raised = [jnp.exp(r - top) for r in rel]
        inverse = 1.0 / (raised[0] + raised[1] + raised[2] + raised[3])
        alpha = [r * inverse for r in raised]
        recalled = sum(a * n for a, n in zip(alpha, near))
        logit = jnp.sum(hidden * gate, axis=-1, keepdims=True)
        gating = jax.nn.sigmoid(logit)
        apart = recalled - hidden
        mixed_ref[span, :] = (hidden + gating * apart).astype(BF16)
        grad_recalled = gating * grad_mixed
        grad_gating = jnp.sum(grad_mixed * apart, axis=-1, keepdims=True)
        grad_logit = grad_gating * gating * (1.0 - gating)
        grad_alpha = [jnp.sum(grad_recalled * n, axis=-1, keepdims=True) for n in near]
        weighed = sum(a * g for a, g in zip(alpha, grad_alpha))
        grad_rel = [a * (g - weighed) * scale for a, g in zip(alpha, grad_alpha)]
        grad_hidden = grad_mixed - grad_recalled + grad_logit * gate
        grad_hidden = grad_hidden + sum(g * n for g, n in zip(grad_rel, near))
        gh_ref[span, :] = grad_hidden
        gate_grad = gate_grad + jnp.sum(grad_logit * hidden, axis=0, keepdims=True)
    gate_grad_ref[...] = gate_grad
    low = gh_ref[...].astype(BF16)
    low_t = low.T
    for s, pack in enumerate((f0, f1, f2, f3)):
        grad_act = mm_nt(low, pack[D : 2 * D, :])
        pre_ref[s] = (grad_act * slope_ref[s].astype(F32)).astype(BF16)
        (send_ref if s % 2 else keep_ref)[s // 2] = mm(low_t, act_ref[s]).astype(BF16)


FEED_ROWS = D + SLOT + 64


def feed_back_kernel(
    gh_ref, gate_grad_ref, middle_ref, nm_ref, pre_ref, g_ref, t0, t1, t2, t3, f0, f1, f2, f3,
    gm_ref, a0, a1, a2, a3, keep_ref, send_ref,
):
    grad_hidden = gh_ref[...]
    normed_t = nm_ref[...].T
    packs = (f0, f1, f2, f3)
    outer_bias_grad = jnp.sum(grad_hidden, axis=0, keepdims=True)
    grad_nm = jnp.zeros((SEG, D), F32)
    for s, pack in enumerate(packs):
        pay = send_ref if s % 2 else keep_ref
        pay[s // 2, 0:D, :] = mm(normed_t, pre_ref[s]).astype(BF16)
        grad_nm = grad_nm + mm_nt(pre_ref[s], pack[0:D, :])
    xhat, inverse = norm_parts(middle_ref[...])
    gain_grad = jnp.sum(grad_nm * xhat, axis=0, keepdims=True)
    bias_grad = jnp.sum(grad_nm, axis=0, keepdims=True)
    grad_middle = grad_hidden + norm_back(grad_nm, g_ref[...], xhat, inverse)
    gm_ref[...] = grad_middle
    middle_low = grad_middle.astype(BF16)
    zeros = jnp.zeros((59, D), F32)
    for s, (att, grad_att, pack) in enumerate(
        zip((t0, t1, t2, t3), (a0, a1, a2, a3), packs)
    ):
        pay = send_ref if s % 2 else keep_ref
        pay[s // 2, D : D + SLOT, :] = mm_tn(att[...], middle_low).astype(BF16)
        grad_att[...] = mm_nt(middle_low, pack[2 * D :, :]).astype(BF16)
        inner_bias_grad = jnp.sum(pre_ref[s].astype(F32), axis=0, keepdims=True)
        rows = jnp.concatenate(
            [inner_bias_grad, gain_grad, bias_grad, outer_bias_grad, gate_grad_ref[...], zeros],
            axis=0,
        )
        pay[s // 2, D + SLOT :, :] = rows.astype(BF16)


HEAD_ROWS = 4 * SLOT + 64


def attend_back_kernel(
    keys_ref, table_ref, probs_ref, qc_ref, qp_ref, kr_ref, vr_ref, pk_ref, ga_ref,
    pay_ref, both_ref, gq_ref,
):
    half = SEG // 2
    across = lax.broadcasted_iota(jnp.int32, (half, half), 1)
    down = lax.broadcasted_iota(jnp.int32, (half, half), 0)
    swap = jnp.where(across + down == half - 1, 1.0, 0.0).astype(BF16)

    def flip(values):
        return jnp.concatenate([mm(swap, values[half:]), mm(swap, values[:half])], axis=0)

    keys_in = keys_ref[...]
    normed = keys_ref[MEM:, :]
    grad_v = jnp.zeros((SLOT, KEYS), F32)
    grad_k = jnp.zeros((SLOT, KEYS), F32)
    grad_p = jnp.zeros((SLOT, KEYS), F32)
    grad_c = jnp.zeros((SEG, SLOT), F32)
    grad_place = jnp.zeros((SEG, SLOT), F32)
    qp_flip = flip(qp_ref[...]).astype(BF16)
    for h in range(2):
        probs = probs_ref[h]
        grad_out = of_head(ga_ref[...], h)
        grad_probs = mm_nt(grad_out, vr_ref[...])
        wide = probs.astype(F32)
        weighed = jnp.sum(wide * grad_probs, axis=-1, keepdims=True)
        grad_scores = (wide * (grad_probs - weighed)).astype(BF16)
        grad_v = grad_v + mm_tn(grad_out, probs)
        grad_k = grad_k + mm_tn(of_head(qc_ref[...], h), grad_scores)
        grad_c = grad_c + mm(grad_scores, of_head(kr_ref[...], h))
        turned = pltpu.roll(flip(grad_scores), 0, 1, stride=1, stride_axis=0).astype(BF16)
        grad_place = grad_place + mm(turned, of_head(pk_ref[...], h))
        grad_p = grad_p + mm_tn(of_head(qp_flip, h), turned)
    grad_v = grad_v.astype(BF16)
    grad_k = (grad_k * SCALE).astype(BF16)
    grad_p = (grad_p * SCALE).astype(BF16)
    grad_c = grad_c * SCALE
    grad_place = grad_place * SCALE
    high = grad_place.astype(BF16)
    rest = (grad_place - high.astype(F32)).astype(BF16)
    grad_q = (grad_c + flip(high) + flip(rest)).astype(BF16)
    gq_ref[...] = grad_q
    both_ref[0:SLOT, :] = grad_k
    both_ref[SLOT:, :] = grad_v
    pay_ref[0:SLOT, :] = mm_tn(grad_q, normed).astype(BF16)
    pay_ref[SLOT : 3 * SLOT, :] = mm(both_ref[...], keys_in).astype(BF16)
    pay_ref[3 * SLOT : 4 * SLOT, :] = mm(grad_p, table_ref[...]).astype(BF16)
    biases = jnp.concatenate(
        [
            jnp.sum(grad_c, axis=0, keepdims=True),
            jnp.sum(grad_place, axis=0, keepdims=True),
            jnp.zeros((1, D - 2 * SLOT), F32),
        ],
        axis=1,
    )
    pay_ref[4 * SLOT :, :] = jnp.concatenate([biases, jnp.zeros((63, D), F32)], axis=0).astype(
        BF16
    )


def input_kernel(
    place_ref, x_ref, m0, m1, m2, m3, gm_ref, g_ref, both_0, both_1, both_2, both_3,
    gq_0, gq_1, gq_2, gq_3, h0, h1, h2, h3,
    grad_ref, vectors_ref,
    total_ref,
):
    me = place_ref[0]
    packs = (h0, h1, h2, h3)
    total = jnp.zeros((KEYS, D), F32)
    for both, pack in zip((both_0, both_1, both_2, both_3), packs):
        total = total + mm_tt(both[...], key_value_of(pack))
    total_ref[...] = total
    grad = total_ref[MEM:, :]
    for gq, pack in zip((gq_0, gq_1, gq_2, gq_3), packs):
        grad = grad + mm_nt(gq[...], query_of(pack))
    xhat, inverse = norm_parts(x_ref[...].astype(F32))
    grad_ref[...] = gm_ref[...] + norm_back(grad, g_ref[...], xhat, inverse)
    gain_grad = jnp.sum(grad * xhat, axis=0, keepdims=True)
    bias_grad = jnp.sum(grad, axis=0, keepdims=True) + jnp.sum(
        total_ref[:MEM, :], axis=0, keepdims=True
    )
    for k, block in enumerate((m0, m1, m2, m3)):
        seen, _ = norm_parts(block[...].astype(F32))
        start = pl.multiple_of((me ^ k) * SLOT, SLOT)
        gain_grad = gain_grad + jnp.sum(
            total_ref[pl.ds(start, SLOT), :] * seen, axis=0, keepdims=True
        )
    vectors_ref[...] = jnp.concatenate([gain_grad, bias_grad, jnp.zeros((6, D), F32)], axis=0)


def swap_with(values, axis, k):
    n = lax.axis_size(axis)
    return lax.ppermute(values, axis, [(i, i ^ k) for i in range(n)])


def add_low(*terms):
    return sum(t.astype(F32) for t in terms).astype(BF16)


def turn(values, axis):
    return lax.all_to_all(values, axis, split_axis=0, concat_axis=0, tiled=True)


def by_steps():
    return lax.axis_size("dp") == 8


def dp_bit():
    return lax.axis_index("dp") % 2


def part_of(values, index, count):
    size = values.shape[0] // count
    return lax.dynamic_slice_in_dim(values, index * size, size)


def halve(values):
    if not by_steps():
        return values
    bit = dp_bit()
    got = swap_with(part_of(values, 1 - bit, 2), "dp", 1)
    return add_low(part_of(values, bit, 2), got)


def quarter(values):
    if not by_steps():
        n = lax.axis_size("dp")
        got = turn(values.reshape(n, values.shape[0] // n, D), "dp")
        return jnp.sum(got.astype(F32), axis=0).astype(BF16)
    z = lax.axis_index("dp") // 2
    got = [swap_with(part_of(values, z ^ k, 4), "dp", 2 * k) for k in (3, 2, 1)]
    return add_low(part_of(values, z, 4), *got)


def spread(part):
    if not by_steps():
        n = lax.axis_size("dp")
        return turn(jnp.broadcast_to(part[None], (n,) + part.shape), "dp").reshape(-1, D)
    z = lax.axis_index("dp") // 2
    parts = [part] + [swap_with(part, "dp", 2 * k) for k in (1, 2, 3)]
    low, high = z % 2 == 0, z < 2
    return jnp.concatenate(
        [
            jnp.where(
                high,
                jnp.where(low, parts[j], parts[j ^ 1]),
                jnp.where(low, parts[j ^ 2], parts[j ^ 3]),
            )
            for j in range(4)
        ],
        axis=0,
    )


def both_halves(half):
    if not by_steps():
        return half[: half.shape[0] // 2], half[half.shape[0] // 2 :]
    other = swap_with(half, "dp", 1)
    first = dp_bit() == 0
    return jnp.where(first, half, other), jnp.where(first, other, half)


def outer_out_kernel(a_ref, b_ref, out_ref):
    full = jnp.concatenate([a_ref[...], b_ref[...]], axis=0)
    out_ref[...] = full.T.astype(F32)


def inner_out_kernel(a_ref, b_ref, inner_ref, output_ref, rows_ref):
    half = FEED_ROWS // 2
    inner_ref[0:half, :] = a_ref[...].astype(F32)
    inner_ref[half:, :] = b_ref[: D - half, :].astype(F32)
    output_ref[...] = b_ref[D - half : D - half + SLOT, :].astype(F32)
    rows_ref[...] = b_ref[D - half + SLOT :, :].astype(F32)[:8]


def head_out_kernel(a_ref, b_ref, q_ref, k_ref, v_ref, p_ref, rows_ref):
    full = jnp.concatenate([a_ref[...], b_ref[...]], axis=0)
    for n, ref in enumerate((q_ref, k_ref, v_ref, p_ref)):
        ref[...] = full[n * SLOT : (n + 1) * SLOT].T.astype(F32)
    rows_ref[...] = full[4 * SLOT : 4 * SLOT + 16].astype(F32)[:8]


def all_shards(values):
    one = swap_with(values, "mp", 1)
    two = swap_with(values, "mp", 2)
    three = swap_with(two, "mp", 1)
    return [values, one, two, three]


def local(
    block_input,
    memory,
    cotangent,
    neighbour_table,
    requests,
    counts,
    neighbour_slots,
    memory_lengths,
    document_lengths,
    first_gain,
    first_bias,
    query_weight,
    key_weight,
    value_weight,
    position_weight,
    content_bias,
    position_bias,
    output_weight,
    second_gain,
    second_bias,
    inner_weight,
    inner_bias,
    outer_weight,
    outer_bias,
    gate_weight,
):
    place = lax.axis_index("mp").astype(jnp.int32).reshape(1)
    data_size = lax.axis_size("dp")
    capacity = requests.shape[1]
    row = lambda v: v.reshape(1, -1)
    g1, b1, g2, b2 = row(first_gain), row(first_bias), row(second_gain), row(second_bias)
    low_square = shape((SEG, D), BF16)
    block = shape((SLOT, D), BF16)

    wanted = turn(requests, "dp").reshape(requests.shape)

    *mem_own, head_pack = call(
        start_kernel,
        (block, block, block, block, shape((HEAD_PACK, D), BF16)),
        [
            place, memory, query_weight, key_weight, value_weight, position_weight,
            row(inner_bias), row(content_bias), row(position_bias),
        ],
        smem=1,
        after=[wanted],
    )
    mem = [mem_own[0]] + [swap_with(mem_own[k], "mp", k) for k in (1, 2, 3)]
    heads = all_shards(head_pack)
    found = jnp.take(neighbour_table, wanted, axis=0, mode="clip")
    fetched = turn(found, "dp").reshape(data_size * capacity, D)
    (feed_pack,) = call(
        feed_pack_kernel,
        (shape((FEED_PACK, D), BF16),),
        [inner_weight, outer_weight, output_weight],
        after=[found],
    )
    feeds = all_shards(feed_pack)
    table = position_table()

    (keys_in,) = call(
        memory_kernel, (shape((KEYS, D), BF16),), [place, *mem, block_input, g1, b1],
        smem=1, after=[feed_pack], us=0,
    )

    def attend(n, after):
        slot = lambda rows: shape((rows, SLOT), BF16)
        return call(
            attend_kernel,
            (
                shape((2, SEG, KEYS), BF16),
                slot(SEG), slot(SEG), slot(KEYS), slot(KEYS), slot(KEYS), slot(SEG),
            ),
            [place, memory_lengths, document_lengths, keys_in, table, heads[n]],
            scratch=[pltpu.VMEM((SEG, KEYS), F32)],
            smem=3,
            after=after,
            us=30,
        )

    saved = []
    for n in range(4):
        saved.append(attend(n, [saved[-1][-1]] if saved else []))
    attended = [v[-1] for v in saved]

    square = shape((SEG, D), F32)
    units = shape((4, SEG, D), BF16)
    middle, hidden, normed_middle, activation, slope = call(
        feed_kernel,
        (square, square, low_square, units, units),
        [block_input, *attended, g2, b2, *heads, *feeds, row(outer_bias)],
        us=60,
    )

    pair = shape((2, D, D), BF16)

    mixed, grad_hidden, grad_gate, outer_keep, outer_send, grad_pre = call(
        mix_kernel,
        (low_square, square, shape((1, D), F32), pair, pair, units),
        [
            place, document_lengths, fetched, neighbour_slots, cotangent, hidden,
            row(gate_weight), activation, slope, *feeds,
        ],
        smem=2,
        us=14,
    )
    slot_grad = shape((SEG, SLOT), BF16)
    inner_pair = shape((2, FEED_ROWS, D), BF16)
    grad_middle, *grad_att, inner_keep, inner_send = call(
        feed_back_kernel,
        (square, *[slot_grad] * 4, inner_pair, inner_pair),
        [grad_hidden, grad_gate, middle, normed_middle, grad_pre, g2, *attended, *feeds],
        us=9,
    )
    outer_two = add_low(outer_keep, swap_with(outer_send, "mp", 1))
    outer_far = swap_with(outer_two[1], "mp", 2)

    def attend_back(n, after):
        return call(
            attend_back_kernel,
            (shape((HEAD_ROWS, D), BF16), shape((2 * SLOT, KEYS), BF16), shape((SEG, SLOT), BF16)),
            [keys_in, table, *saved[n][:-1], grad_att[n]],
            us=9,
            after=after,
        )

    pay_3, both_3, gq_3 = attend_back(3, [outer_two])
    inner_two = add_low(inner_keep, swap_with(inner_send, "mp", 1))
    inner_far = swap_with(inner_two[1], "mp", 2)
    pay_2, both_2, gq_2 = attend_back(2, [inner_two, pay_3])
    head_two = add_low(pay_2, swap_with(pay_3, "mp", 1))
    head_far = swap_with(head_two, "mp", 2)
    outer_sum = add_low(outer_two[0], outer_far)
    pay_1, both_1, gq_1 = attend_back(1, [head_two, outer_sum])
    outer_half = halve(outer_sum)
    inner_sum = add_low(inner_two[0], inner_far)
    pay_0, both_0, gq_0 = attend_back(0, [pay_1, outer_half, inner_sum])
    outer_part = quarter(outer_half)
    inner_half = halve(inner_sum)
    head_sum = add_low(add_low(pay_0, swap_with(pay_1, "mp", 1)), head_far)

    input_grad, vectors = call(
        input_kernel,
        (square, shape((8, D), F32)),
        [
            place, block_input, *mem, grad_middle, g1, both_0, both_1, both_2, both_3,
            gq_0, gq_1, gq_2, gq_3, *heads,
        ],
        scratch=[pltpu.VMEM((KEYS, D), F32)],
        smem=1,
        after=[outer_part, inner_half, head_sum],
        us=6,
    )
    head_half = halve(head_sum)
    outer_halves = both_halves(spread(outer_part))
    inner_part = quarter(inner_half)
    head_part = quarter(head_half)
    inner_halves = both_halves(spread(inner_part))
    head_halves = both_halves(spread(head_part))
    (outer_grad,) = call(outer_out_kernel, (square,), outer_halves)
    eight = shape((8, D), F32)
    inner_grad, output_grad, rows = call(
        inner_out_kernel, (square, shape((SLOT, D), F32), eight), inner_halves
    )
    weight = shape((D, SLOT), F32)
    query_grad, key_grad, value_grad, place_grad, head_rows = call(
        head_out_kernel, (weight, weight, weight, weight, eight), head_halves
    )

    vectors = vectors + swap_with(vectors, "mp", 1)
    vectors = vectors + swap_with(vectors, "mp", 2)
    if by_steps():
        vectors = vectors + swap_with(vectors, "dp", 1)
        vectors = vectors + swap_with(vectors, "dp", 2)
        vectors = vectors + swap_with(vectors, "dp", 4)
    else:
        vectors = jnp.sum(turn(jnp.broadcast_to(vectors[None], (data_size, 8, D)), "dp"), axis=0)
    return (
        mixed,
        input_grad,
        vectors[0],
        vectors[1],
        query_grad,
        key_grad,
        value_grad,
        place_grad,
        head_rows[0, :SLOT],
        head_rows[0, SLOT : 2 * SLOT],
        output_grad,
        rows[1],
        rows[2],
        inner_grad,
        rows[0],
        outer_grad,
        rows[3],
        rows[4],
    )


def solution(mesh):
    return jax.shard_map(
        local,
        mesh=mesh,
        in_specs=(
            P(("dp", "mp"), None),
            P("dp", "mp", None),
            P(("dp", "mp"), None),
            P("dp", None),
            P(("dp", "mp"), None),
            P(("dp", "mp")),
            P(("dp", "mp"), None),
            P("dp"),
            P("dp"),
            P(),
            P(),
            P(None, "mp"),
            P(None, "mp"),
            P(None, "mp"),
            P(None, "mp"),
            P("mp"),
            P("mp"),
            P("mp", None),
            P(),
            P(),
            P(None, "mp"),
            P("mp"),
            P("mp", None),
            P(),
            P(),
        ),
        out_specs=(
            P(("dp", "mp"), None),
            P(("dp", "mp"), None),
            P(),
            P(),
            P(None, "mp"),
            P(None, "mp"),
            P(None, "mp"),
            P(None, "mp"),
            P("mp"),
            P("mp"),
            P("mp", None),
            P(),
            P(),
            P(None, "mp"),
            P("mp"),
            P("mp", None),
            P(),
            P(),
        ),
        check_vma=False,
    )
```

```python
import math

import jax
import jax.numpy as jnp
import numpy as np
from jax import lax
from jax.experimental import pallas as pl
from jax.experimental.pallas import tpu as pltpu
from jax.sharding import PartitionSpec as P

D = 512
HD = 64
SEG = 512
MEM = 512
KEYS = 1024
SLOT = 128
EPS = 1e-05
F32 = jnp.float32
BF16 = jnp.bfloat16
GELU_C = math.sqrt(2.0 / math.pi)
SCALE = HD ** (-0.5)
VMEM = pl.BlockSpec(memory_space=pltpu.VMEM)
SMEM = pl.BlockSpec(memory_space=pltpu.SMEM)
ANY = pl.BlockSpec(memory_space=pl.ANY)


def position_table():
    distance = (KEYS - 1 - np.arange(KEYS)).astype(np.float32)
    exponent = np.arange(0, D, 2).astype(np.float32) / np.float32(D)
    angles = distance[:, None] * np.exp(np.float32(-math.log(10000.0)) * exponent)[None, :]
    table = np.concatenate([np.sin(angles), np.cos(angles)], axis=1).astype(np.float32)
    return jnp.asarray(table).astype(BF16)


def call(body, outs, ins, us=1, scratch=(), smem=0, after=(), vmem=56):
    count = len(ins)

    def run(*refs):
        body(*refs[:count], *refs[count + len(after) :])

    nbytes = sum(a.size * a.dtype.itemsize for a in ins)
    return pl.pallas_call(
        run,
        out_shape=outs,
        in_specs=[SMEM] * smem + [VMEM] * (count - smem) + [ANY] * len(after),
        out_specs=jax.tree.map(lambda _: VMEM, outs),
        scratch_shapes=list(scratch),
        compiler_params=pltpu.CompilerParams(vmem_limit_bytes=vmem * 2**20),
        cost_estimate=pl.CostEstimate(flops=us * 10**9, bytes_accessed=nbytes, transcendentals=0),
    )(*ins, *after)


def shape(dims, dtype):
    return jax.ShapeDtypeStruct(dims, dtype)


def mm(a, b):
    return jnp.dot(a, b, preferred_element_type=F32)


def mm_nt(a, b):
    return lax.dot_general(a, b, (((1,), (1,)), ((), ())), preferred_element_type=F32)


def mm_tn(a, b):
    return lax.dot_general(a, b, (((0,), (0,)), ((), ())), preferred_element_type=F32)


def mm_tt(a, b):
    return lax.dot_general(a, b, (((0,), (1,)), ((), ())), preferred_element_type=F32)


def norm_parts(values):
    average = jnp.mean(values, axis=-1, keepdims=True)
    centred = values - average
    spread = jnp.mean(centred * centred, axis=-1, keepdims=True)
    inverse = lax.rsqrt(spread + EPS)
    return centred * inverse, inverse


def norm_back(grad, gain, xhat, inverse):
    scaled = grad * gain
    return inverse * (
        scaled
        - jnp.mean(scaled, axis=-1, keepdims=True)
        - xhat * jnp.mean(scaled * xhat, axis=-1, keepdims=True)
    )


def head_lanes(rows, h):
    lane = lax.broadcasted_iota(jnp.int32, (rows, SLOT), 1)
    return (lane // HD) == h


def of_head(values, h):
    return jnp.where(head_lanes(values.shape[0], h), values, jnp.zeros_like(values))


HEAD_PACK = D + 16
FEED_PACK = 2 * D + SLOT


def query_of(pack):
    return pack[0:D, 0:SLOT]


def key_value_of(pack):
    return pack[0:D, SLOT : 3 * SLOT]


def place_of(pack):
    return pack[0:D, 3 * SLOT : 4 * SLOT]


def start_kernel(
    place_ref, mem_ref, wq, wk, wv, wp, ib_ref, cb_ref, pb_ref,
    m0, m1, m2, m3, pack_ref,
):
    me = place_ref[0]
    for k, block in enumerate((m0, m1, m2, m3)):
        block[...] = mem_ref[me ^ k]
    for n, w in enumerate((wq, wk, wv, wp)):
        pack_ref[0:D, n * SLOT : (n + 1) * SLOT] = w[...]
    biases = jnp.concatenate([cb_ref[...], pb_ref[...]] * 2, axis=1)
    high = biases.astype(BF16).astype(F32)
    middle = (biases - high).astype(BF16).astype(F32)
    rows = jnp.concatenate(
        [ib_ref[...].astype(F32), high, middle, biases - high - middle, jnp.zeros((12, D), F32)],
        axis=0,
    )
    pack_ref[D:, :] = rows.astype(BF16)


def feed_pack_kernel(wi, wu, wo, pack_ref):
    pack_ref[0:D, :] = wi[...]
    pack_ref[D : 2 * D, :] = wu[...]
    pack_ref[2 * D :, :] = wo[...]


def memory_kernel(place_ref, m0, m1, m2, m3, x_ref, g_ref, b_ref, keys_ref):
    me = place_ref[0]
    for k, block in enumerate((m0, m1, m2, m3)):
        xhat, _ = norm_parts(block[...].astype(F32))
        start = pl.multiple_of((me ^ k) * SLOT, SLOT)
        keys_ref[pl.ds(start, SLOT), :] = (xhat * g_ref[...] + b_ref[...]).astype(BF16)
    xhat, _ = norm_parts(x_ref[...].astype(F32))
    keys_ref[MEM:, :] = (xhat * g_ref[...] + b_ref[...]).astype(BF16)


def attend_kernel(
    place_ref, mem_ref, doc_ref, keys_ref, table_ref, pack,
    probs_ref, qc_ref, qp_ref, kr_ref, vr_ref, pk_ref, att_ref,
    bias_ref,
):
    row = place_ref[0]
    low = MEM - mem_ref[row]
    high = MEM + doc_ref[row]
    place_k = lax.broadcasted_iota(jnp.int32, (SEG, KEYS), 1)
    place_q = lax.broadcasted_iota(jnp.int32, (SEG, KEYS), 0)
    live = (place_k >= low) & (place_k <= MEM + place_q) & (place_k < high)
    bias_ref[...] = jnp.where(live, 0.0, -1e30)
    small = pack[D:, :].astype(F32)
    offsets = small[1:2] + small[2:3] + small[3:4]
    query = mm(keys_ref[MEM:, :], query_of(pack))
    qc_ref[...] = (query + offsets[:, :SLOT]).astype(BF16)
    qp_ref[...] = (query + offsets[:, SLOT : 2 * SLOT]).astype(BF16)
    both = mm(keys_ref[...], key_value_of(pack)).astype(BF16)
    kr_ref[...] = both[:, :SLOT]
    vr_ref[...] = both[:, SLOT:]
    pk_ref[...] = mm(table_ref[...], place_of(pack)).astype(BF16)
    parts = []
    for h in range(2):
        content = mm_nt(of_head(qc_ref[...], h), kr_ref[...])
        place = mm_nt(of_head(qp_ref[...], h), pk_ref[...])
        place = pltpu.roll(place, KEYS - SEG + 1, 1, stride=1, stride_axis=0)
        scores = (content + place) * SCALE + bias_ref[...]
        largest = jnp.max(scores, axis=-1, keepdims=True)
        raised = jnp.exp(scores - largest)
        total = jnp.sum(raised, axis=-1, keepdims=True)
        probs = (raised * (1.0 / total)).astype(BF16)
        probs_ref[h] = probs
        parts.append(mm(probs, vr_ref[...]))
    att_ref[...] = jnp.where(head_lanes(SEG, 0), parts[0], parts[1]).astype(BF16)


def feed_kernel(
    x_ref, t0, t1, t2, t3, g_ref, b_ref, h0, h1, h2, h3, f0, f1, f2, f3, ob_ref,
    middle_ref, hidden_ref, nm_ref, act_ref, slope_ref,
):
    middle = x_ref[...].astype(F32)
    packs = (f0, f1, f2, f3)
    for att, pack in zip((t0, t1, t2, t3), packs):
        middle = middle + mm(att[...], pack[2 * D :, :])
    middle_ref[...] = middle
    xhat, _ = norm_parts(middle)
    normed = (xhat * g_ref[...] + b_ref[...]).astype(BF16)
    nm_ref[...] = normed
    hidden = middle + ob_ref[...]
    for s, (small, pack) in enumerate(zip((h0, h1, h2, h3), packs)):
        pre = mm(normed, pack[0:D, :]) + small[D:, :].astype(F32)[0:1]
        square = pre * pre
        bend = jnp.tanh(GELU_C * (pre + 0.044715 * (pre * square)))
        act = (0.5 * pre * (1.0 + bend)).astype(BF16)
        slope = 0.5 * (1.0 + bend) + (0.5 * GELU_C) * pre * (1.0 - bend * bend) * (
            1.0 + (3 * 0.044715) * square
        )
        act_ref[s] = act
        slope_ref[s] = slope.astype(BF16)
        hidden = hidden + mm(act, pack[D : 2 * D, :])
    hidden_ref[...] = hidden


def mix_kernel(
    place_ref, doc_ref, fetched, slots_ref, cot_ref, hidden_ref, gate_ref,
    act_ref, slope_ref, f0, f1, f2, f3,
    mixed_ref, gh_ref, gate_grad_ref, keep_ref, send_ref, pre_ref,
):
    total = fetched.shape[0]
    docs = doc_ref[place_ref[0]]
    gate = gate_ref[...]
    scale = 1.0 / math.sqrt(D)
    step = 128
    gate_grad = jnp.zeros((1, D), F32)
    for c in range(SEG // step):
        span = slice(c * step, (c + 1) * step)
        lane = lax.broadcasted_iota(jnp.int32, (step, total), 1)
        near = []
        for j in range(4):
            pick = jnp.where(slots_ref[span, j : j + 1] == lane, 1.0, 0.0).astype(BF16)
            near.append(mm(pick, fetched[...]))
        hidden = hidden_ref[span, :]
        token = c * step + lax.broadcasted_iota(jnp.int32, (step, 1), 0)
        grad_mixed = cot_ref[span, :].astype(F32) * jnp.where(token < docs, 1.0, 0.0)
        rel = [jnp.sum(hidden * n, axis=-1, keepdims=True) * scale for n in near]
        top = jnp.maximum(jnp.maximum(rel[0], rel[1]), jnp.maximum(rel[2], rel[3]))
        raised = [jnp.exp(r - top) for r in rel]
        inverse = 1.0 / (raised[0] + raised[1] + raised[2] + raised[3])
        alpha = [r * inverse for r in raised]
        recalled = sum(a * n for a, n in zip(alpha, near))
        logit = jnp.sum(hidden * gate, axis=-1, keepdims=True)
        gating = jax.nn.sigmoid(logit)
        apart = recalled - hidden
        mixed_ref[span, :] = (hidden + gating * apart).astype(BF16)
        grad_recalled = gating * grad_mixed
        grad_gating = jnp.sum(grad_mixed * apart, axis=-1, keepdims=True)
        grad_logit = grad_gating * gating * (1.0 - gating)
        grad_alpha = [jnp.sum(grad_recalled * n, axis=-1, keepdims=True) for n in near]
        weighed = sum(a * g for a, g in zip(alpha, grad_alpha))
        grad_rel = [a * (g - weighed) * scale for a, g in zip(alpha, grad_alpha)]
        grad_hidden = grad_mixed - grad_recalled + grad_logit * gate
        grad_hidden = grad_hidden + sum(g * n for g, n in zip(grad_rel, near))
        gh_ref[span, :] = grad_hidden
        gate_grad = gate_grad + jnp.sum(grad_logit * hidden, axis=0, keepdims=True)
    gate_grad_ref[...] = gate_grad
    low = gh_ref[...].astype(BF16)
    low_t = low.T
    for s, pack in enumerate((f0, f1, f2, f3)):
        grad_act = mm_nt(low, pack[D : 2 * D, :])
        pre_ref[s] = (grad_act * slope_ref[s].astype(F32)).astype(BF16)
        (send_ref if s % 2 else keep_ref)[s // 2] = mm(low_t, act_ref[s]).astype(BF16)


FEED_ROWS = D + SLOT + 16


def feed_back_kernel(
    gh_ref, gate_grad_ref, middle_ref, nm_ref, pre_ref, g_ref, t0, t1, t2, t3, f0, f1, f2, f3,
    gm_ref, a0, a1, a2, a3, keep_ref, send_ref,
):
    grad_hidden = gh_ref[...]
    normed_t = nm_ref[...].T
    packs = (f0, f1, f2, f3)
    outer_bias_grad = jnp.sum(grad_hidden, axis=0, keepdims=True)
    grad_nm = jnp.zeros((SEG, D), F32)
    for s, pack in enumerate(packs):
        pay = send_ref if s % 2 else keep_ref
        pay[s // 2, 0:D, :] = mm(normed_t, pre_ref[s]).astype(BF16)
        grad_nm = grad_nm + mm_nt(pre_ref[s], pack[0:D, :])
    xhat, inverse = norm_parts(middle_ref[...])
    gain_grad = jnp.sum(grad_nm * xhat, axis=0, keepdims=True)
    bias_grad = jnp.sum(grad_nm, axis=0, keepdims=True)
    grad_middle = grad_hidden + norm_back(grad_nm, g_ref[...], xhat, inverse)
    gm_ref[...] = grad_middle
    middle_low = grad_middle.astype(BF16)
    zeros = jnp.zeros((11, D), F32)
    for s, (att, grad_att, pack) in enumerate(
        zip((t0, t1, t2, t3), (a0, a1, a2, a3), packs)
    ):
        pay = send_ref if s % 2 else keep_ref
        pay[s // 2, D : D + SLOT, :] = mm_tn(att[...], middle_low).astype(BF16)
        grad_att[...] = mm_nt(middle_low, pack[2 * D :, :]).astype(BF16)
        inner_bias_grad = jnp.sum(pre_ref[s].astype(F32), axis=0, keepdims=True)
        rows = jnp.concatenate(
            [inner_bias_grad, gain_grad, bias_grad, outer_bias_grad, gate_grad_ref[...], zeros],
            axis=0,
        )
        pay[s // 2, D + SLOT :, :] = rows.astype(BF16)


HEAD_ROWS = 4 * SLOT + 16


def attend_back_kernel(
    keys_ref, table_ref, probs_ref, qc_ref, qp_ref, kr_ref, vr_ref, pk_ref, ga_ref,
    pay_ref, both_ref, gq_ref,
):
    half = SEG // 2
    across = lax.broadcasted_iota(jnp.int32, (half, half), 1)
    down = lax.broadcasted_iota(jnp.int32, (half, half), 0)
    swap = jnp.where(across + down == half - 1, 1.0, 0.0).astype(BF16)

    def flip(values):
        return jnp.concatenate([mm(swap, values[half:]), mm(swap, values[:half])], axis=0)

    keys_in = keys_ref[...]
    normed = keys_ref[MEM:, :]
    grad_v = jnp.zeros((SLOT, KEYS), F32)
    grad_k = jnp.zeros((SLOT, KEYS), F32)
    grad_p = jnp.zeros((SLOT, KEYS), F32)
    grad_c = jnp.zeros((SEG, SLOT), F32)
    grad_place = jnp.zeros((SEG, SLOT), F32)
    qp_flip = flip(qp_ref[...]).astype(BF16)
    for h in range(2):
        probs = probs_ref[h]
        grad_out = of_head(ga_ref[...], h)
        grad_probs = mm_nt(grad_out, vr_ref[...])
        wide = probs.astype(F32)
        weighed = jnp.sum(wide * grad_probs, axis=-1, keepdims=True)
        grad_scores = (wide * (grad_probs - weighed)).astype(BF16)
        grad_v = grad_v + mm_tn(grad_out, probs)
        grad_k = grad_k + mm_tn(of_head(qc_ref[...], h), grad_scores)
        grad_c = grad_c + mm(grad_scores, of_head(kr_ref[...], h))
        turned = pltpu.roll(flip(grad_scores), 0, 1, stride=1, stride_axis=0).astype(BF16)
        grad_place = grad_place + mm(turned, of_head(pk_ref[...], h))
        grad_p = grad_p + mm_tn(of_head(qp_flip, h), turned)
    grad_v = grad_v.astype(BF16)
    grad_k = (grad_k * SCALE).astype(BF16)
    grad_p = (grad_p * SCALE).astype(BF16)
    grad_c = grad_c * SCALE
    grad_place = grad_place * SCALE
    high = grad_place.astype(BF16)
    rest = (grad_place - high.astype(F32)).astype(BF16)
    grad_q = (grad_c + flip(high) + flip(rest)).astype(BF16)
    gq_ref[...] = grad_q
    both_ref[0:SLOT, :] = grad_k
    both_ref[SLOT:, :] = grad_v
    pay_ref[0:SLOT, :] = mm_tn(grad_q, normed).astype(BF16)
    pay_ref[SLOT : 3 * SLOT, :] = mm(both_ref[...], keys_in).astype(BF16)
    pay_ref[3 * SLOT : 4 * SLOT, :] = mm(grad_p, table_ref[...]).astype(BF16)
    biases = jnp.concatenate(
        [
            jnp.sum(grad_c, axis=0, keepdims=True),
            jnp.sum(grad_place, axis=0, keepdims=True),
            jnp.zeros((1, D - 2 * SLOT), F32),
        ],
        axis=1,
    )
    pay_ref[4 * SLOT :, :] = jnp.concatenate([biases, jnp.zeros((15, D), F32)], axis=0).astype(
        BF16
    )


def input_kernel(
    place_ref, x_ref, m0, m1, m2, m3, gm_ref, g_ref, both_0, both_1, both_2, both_3,
    gq_0, gq_1, gq_2, gq_3, h0, h1, h2, h3,
    grad_ref, vectors_ref,
    total_ref,
):
    me = place_ref[0]
    packs = (h0, h1, h2, h3)
    total = jnp.zeros((KEYS, D), F32)
    for both, pack in zip((both_0, both_1, both_2, both_3), packs):
        total = total + mm_tt(both[...], key_value_of(pack))
    total_ref[...] = total
    grad = total_ref[MEM:, :]
    for gq, pack in zip((gq_0, gq_1, gq_2, gq_3), packs):
        grad = grad + mm_nt(gq[...], query_of(pack))
    xhat, inverse = norm_parts(x_ref[...].astype(F32))
    grad_ref[...] = gm_ref[...] + norm_back(grad, g_ref[...], xhat, inverse)
    gain_grad = jnp.sum(grad * xhat, axis=0, keepdims=True)
    bias_grad = jnp.sum(grad, axis=0, keepdims=True) + jnp.sum(
        total_ref[:MEM, :], axis=0, keepdims=True
    )
    for k, block in enumerate((m0, m1, m2, m3)):
        seen, _ = norm_parts(block[...].astype(F32))
        start = pl.multiple_of((me ^ k) * SLOT, SLOT)
        gain_grad = gain_grad + jnp.sum(
            total_ref[pl.ds(start, SLOT), :] * seen, axis=0, keepdims=True
        )
    vectors_ref[...] = jnp.concatenate([gain_grad, bias_grad, jnp.zeros((6, D), F32)], axis=0)


def swap_with(values, axis, k):
    n = lax.axis_size(axis)
    return lax.ppermute(values, axis, [(i, i ^ k) for i in range(n)])


def turn(values, axis):
    return lax.all_to_all(values, axis, split_axis=0, concat_axis=0, tiled=True)


def by_steps():
    return lax.axis_size("dp") == 8


def when(values, after):
    return lax.optimization_barrier((values, after))[0]


def wide(*terms):
    return sum(t.astype(F32) for t in terms)


def part_of(values, index, count):
    size = values.shape[0] // count
    return lax.dynamic_slice_in_dim(values, index * size, size)


def in_order(place_ref, own, other, half):
    first = place_ref[1] == 0
    top = jnp.where(first, own[:half, :], other[:half, :])
    bottom = jnp.where(first, other[:half, :], own[:half, :])
    vectors = None
    if own.shape[0] > half:
        vectors = own[half:, :].astype(F32) + other[half:, :].astype(F32)
    return top, bottom, vectors


def outer_out_kernel(place_ref, own, other, out_ref):
    top, bottom, _ = in_order(place_ref, own, other, D // 2)
    out_ref[...] = jnp.concatenate([top, bottom], axis=0).T.astype(F32)


def inner_out_kernel(place_ref, own, other, inner_ref, output_ref, *rows_refs):
    half = (D + SLOT) // 2
    top, bottom, vectors = in_order(place_ref, own, other, half)
    inner_ref[0:half, :] = top.astype(F32)
    inner_ref[half:, :] = bottom[: D - half].astype(F32)
    output_ref[...] = bottom[D - half :].astype(F32)
    for n, ref in enumerate(rows_refs):
        ref[...] = vectors[n : n + 1]


def head_out_kernel(place_ref, own, other, q_ref, k_ref, v_ref, p_ref, *rows_refs):
    top, bottom, vectors = in_order(place_ref, own, other, D // 2)
    full = jnp.concatenate([top, bottom], axis=0)
    for n, ref in enumerate((q_ref, k_ref, v_ref, p_ref)):
        ref[...] = full[n * SLOT : (n + 1) * SLOT].T.astype(F32)
    content, place, gain, bias = rows_refs
    content[...] = vectors[0:1, :SLOT]
    place[...] = vectors[0:1, SLOT : 2 * SLOT]
    gain[...] = vectors[1:2]
    bias[...] = vectors[2:3]


class Summed:
    def __init__(self, place, rows, tail):
        self.place, self.rows, self.tail = place, rows, tail
        self.level = 0
        self.vectors = None

    def send_half(self, terms):
        bit = self.place[1 + self.level]
        self.kept = [part_of(t, bit, 2) for t in terms]
        sent = wide(*(part_of(t, 1 - bit, 2) for t in terms)).astype(BF16)
        self.got = swap_with(sent, "dp", 2**self.level)
        self.level += 1
        return sent

    def first(self, terms, after):
        terms = when(terms, after)
        if self.tail:
            self.vectors = wide(*(t[self.rows :] for t in terms)).astype(BF16)
        return self.send_half([t[: self.rows] for t in terms])

    def down(self, after):
        return self.send_half([*self.kept, when(self.got, after)])

    def send_back(self, part):
        self.level -= 1
        self.part = part
        message = part if self.vectors is None else jnp.concatenate([part, self.vectors], axis=0)
        self.got = swap_with(message, "dp", 2**self.level)
        return message

    def turn(self, after, vec=()):
        part = wide(*self.kept, when(self.got, after)).astype(BF16)
        if vec:
            lines = wide(*vec)[0:2].astype(BF16)
            self.vectors = jnp.concatenate([self.vectors[0:1], lines, self.vectors[3:]], axis=0)
        return self.send_back(part)

    def cross(self, after):
        part = wide(*self.kept, when(self.got, after)).astype(BF16)
        rows = part.shape[0] // 2
        self.kept, self.got = part[:rows], swap_with(part[rows:], "mp", 2)
        return part

    def turn_near(self, after):
        return self.send_back(wide(self.kept, when(self.got, after)).astype(BF16))

    def joined(self, got):
        rows = self.part.shape[0]
        low = self.place[1 + self.level] == 0
        other = got[:rows]
        if self.vectors is not None:
            self.vectors = wide(self.vectors, got[rows:]).astype(BF16)
        return jnp.concatenate(
            [jnp.where(low, self.part, other), jnp.where(low, other, self.part)], axis=0
        )

    def up(self, after):
        return self.send_back(self.joined(when(self.got, after)))

    def out(self, kernel, outs, after):
        own = self.part
        if self.vectors is not None:
            own = jnp.concatenate([own, self.vectors], axis=0)
        return call(kernel, outs, [self.place, own, self.got], smem=1, after=after)


def dp_sum(values):
    n = lax.axis_size("dp")
    rows = values.shape[0]
    got = turn(values.reshape(n, rows // n, D), "dp")
    part = jnp.sum(got.astype(F32), axis=0).astype(BF16)
    return turn(jnp.broadcast_to(part[None], (n,) + part.shape), "dp").reshape(rows, D)


def dp_vectors(values):
    n = lax.axis_size("dp")
    return jnp.sum(turn(jnp.broadcast_to(values[None], (n,) + values.shape), "dp"), axis=0)


def all_shards(values):
    one = swap_with(values, "mp", 1)
    two = swap_with(values, "mp", 2)
    three = swap_with(two, "mp", 1)
    return [values, one, two, three]


def local(
    block_input,
    memory,
    cotangent,
    neighbour_table,
    requests,
    counts,
    neighbour_slots,
    memory_lengths,
    document_lengths,
    first_gain,
    first_bias,
    query_weight,
    key_weight,
    value_weight,
    position_weight,
    content_bias,
    position_bias,
    output_weight,
    second_gain,
    second_bias,
    inner_weight,
    inner_bias,
    outer_weight,
    outer_bias,
    gate_weight,
):
    data_index = lax.axis_index("dp").astype(jnp.int32)
    place = jnp.stack(
        [lax.axis_index("mp").astype(jnp.int32)] + [data_index // 2**n % 2 for n in range(3)]
    )
    data_size = lax.axis_size("dp")
    capacity = requests.shape[1]
    row = lambda v: v.reshape(1, -1)
    g1, b1, g2, b2 = row(first_gain), row(first_bias), row(second_gain), row(second_bias)
    low_square = shape((SEG, D), BF16)
    block = shape((SLOT, D), BF16)

    wanted = turn(requests, "dp").reshape(requests.shape)

    *mem_own, head_pack = call(
        start_kernel,
        (block, block, block, block, shape((HEAD_PACK, D), BF16)),
        [
            place, memory, query_weight, key_weight, value_weight, position_weight,
            row(inner_bias), row(content_bias), row(position_bias),
        ],
        smem=1,
    )
    mem = [mem_own[0]] + [swap_with(mem_own[k], "mp", k) for k in (1, 2, 3)]
    heads = all_shards(head_pack)
    found = jnp.take(neighbour_table, wanted, axis=0, mode="clip")
    fetched = turn(found, "dp").reshape(data_size * capacity, D)
    (feed_pack,) = call(
        feed_pack_kernel,
        (shape((FEED_PACK, D), BF16),),
        [inner_weight, outer_weight, output_weight],
        after=[found],
    )
    feeds = all_shards(feed_pack)
    table = position_table()

    (keys_in,) = call(
        memory_kernel, (shape((KEYS, D), BF16),), [place, *mem, block_input, g1, b1],
        smem=1, after=[feed_pack], us=0,
    )

    def attend(n, after):
        slot = lambda rows: shape((rows, SLOT), BF16)
        return call(
            attend_kernel,
            (
                shape((2, SEG, KEYS), BF16),
                slot(SEG), slot(SEG), slot(KEYS), slot(KEYS), slot(KEYS), slot(SEG),
            ),
            [place, memory_lengths, document_lengths, keys_in, table, heads[n]],
            scratch=[pltpu.VMEM((SEG, KEYS), F32)],
            smem=3,
            after=after,
            us=30,
        )

    saved = []
    for n in range(4):
        saved.append(attend(n, [saved[-1][-1]] if saved else []))
    attended = [v[-1] for v in saved]

    square = shape((SEG, D), F32)
    units = shape((4, SEG, D), BF16)
    middle, hidden, normed_middle, activation, slope = call(
        feed_kernel,
        (square, square, low_square, units, units),
        [block_input, *attended, g2, b2, *heads, *feeds, row(outer_bias)],
        us=60,
    )

    pair = shape((2, D, D), BF16)

    mixed, grad_hidden, grad_gate, outer_keep, outer_send, grad_pre = call(
        mix_kernel,
        (low_square, square, shape((1, D), F32), pair, pair, units),
        [
            place, document_lengths, fetched, neighbour_slots, cotangent, hidden,
            row(gate_weight), activation, slope, *feeds,
        ],
        smem=2,
        us=14,
        vmem=56,
    )
    slot_grad = shape((SEG, SLOT), BF16)
    inner_pair = shape((2, FEED_ROWS, D), BF16)
    grad_middle, *grad_att, inner_keep, inner_send = call(
        feed_back_kernel,
        (square, *[slot_grad] * 4, inner_pair, inner_pair),
        [grad_hidden, grad_gate, middle, normed_middle, grad_pre, g2, *attended, *feeds],
        us=9,
        vmem=56,
    )
    def attend_back(n, after):
        return call(
            attend_back_kernel,
            (shape((HEAD_ROWS, D), BF16), shape((2 * SLOT, KEYS), BF16), shape((SEG, SLOT), BF16)),
            [keys_in, table, *saved[n][:-1], grad_att[n]],
            us=9,
            after=after,
            vmem=24,
        )

    def two(keep, send, after):
        keep, got = when((keep, swap_with(send, "mp", 1)), after)
        near, far = (wide(keep[n], got[n]).astype(BF16) for n in range(2))
        return near, swap_with(far, "mp", 2)

    steps = by_steps()
    outer = Summed(place, 2 * D, 0)
    keep, got = when((outer_keep, swap_with(outer_send, "mp", 1)), grad_middle)
    if steps:
        both = wide(keep, got).reshape(2, 8, D // 8, D).swapaxes(0, 1).reshape(2 * D, D).astype(BF16)
        at = outer.first([both], [grad_middle])
    else:
        at = outer_near = wide(keep[0], got[0]).astype(BF16)
        outer_far = swap_with(wide(keep[1], got[1]).astype(BF16), "mp", 2)
    pay_3, both_3, gq_3 = attend_back(3, [at])
    inner_near, inner_far = two(inner_keep, inner_send, [gq_3])
    pay_2, both_2, gq_2 = attend_back(2, [inner_near])
    head_far = wide(*when((pay_2, swap_with(pay_3, "mp", 1)), gq_2)).astype(BF16)
    head_got = swap_with(head_far, "mp", 2)
    inner, head = Summed(place, D + SLOT, 1), Summed(place, D, 1)
    eight = shape((8, D), F32)

    def input_back(after):
        return call(
            input_kernel,
            (square, eight),
            [
                place, block_input, *mem, grad_middle, g1, both_0, both_1, both_2, both_3,
                gq_0, gq_1, gq_2, gq_3, *heads,
            ],
            scratch=[pltpu.VMEM((KEYS, D), F32)],
            smem=1,
            after=after,
            us=6,
            vmem=24,
        )

    weight = shape((D, SLOT), F32)
    line, short = shape((1, D), F32), shape((1, SLOT), F32)
    head_outs = (weight,) * 4 + (short, short, line, line)
    inner_outs = (square, shape((SLOT, D), F32)) + (line,) * 5
    if steps:
        at = outer.down([head_far])
        pay_1, both_1, gq_1 = attend_back(1, [at])
        at = outer.down([gq_1])
        pay_0, both_0, gq_0 = attend_back(0, [at])
        at = inner.first([inner_near, inner_far], [gq_0])
        input_grad, vectors = input_back([at])
        at = outer.cross([vectors])
        at = head.first([pay_0, swap_with(pay_1, "mp", 1), head_got], [at])
        at = inner.down([at])
        at = outer.turn_near([at])
        at = head.down([at])
        at = inner.down([at])
        vectors = wide(*when((vectors, swap_with(vectors, "mp", 1)), at))
        at = outer.up([vectors])
        at = head.down([at])
        at = inner.turn([at])
        at = outer.up([at])
        at = head.turn([at], [vectors, swap_with(vectors, "mp", 2)])
        at = inner.up([at])
        at = head.up([at])
        (outer_grad,) = outer.out(outer_out_kernel, (square,), [at])
        at = inner.up([outer_grad])
        at = head.up([at])
        inner_grad, output_grad, *rows = inner.out(inner_out_kernel, inner_outs, [at])
        query_grad, key_grad, value_grad, place_grad, *head_rows = head.out(
            head_out_kernel, head_outs, [inner_grad]
        )
        content_grad, place_bias_grad, gain_grad, bias_grad = (v[0] for v in head_rows)
        rows = [v[0] for v in rows]
    else:
        pay_1, both_1, gq_1 = attend_back(1, [head_far])
        pay_0, both_0, gq_0 = attend_back(0, [gq_1])
        outer = wide(outer_near, outer_far)
        inner = wide(inner_near, inner_far)
        head = wide(pay_0, swap_with(pay_1, "mp", 1), head_got)
        input_grad, vectors = input_back([gq_0])
        vectors = vectors + swap_with(vectors, "mp", 1)
        vectors = dp_vectors(vectors + swap_with(vectors, "mp", 2))
        outer_grad = dp_sum(outer.astype(BF16)).astype(F32).T
        inner_grad = dp_sum(inner[: D + SLOT].astype(BF16)).astype(F32)
        rows = dp_vectors(inner[D + SLOT :])
        inner_grad, output_grad = inner_grad[:D], inner_grad[D:]
        head_rows = dp_vectors(head[4 * SLOT :])
        grads = dp_sum(head[: 4 * SLOT].astype(BF16)).astype(F32)
        query_grad, key_grad, value_grad, place_grad = (
            grads[n * SLOT : (n + 1) * SLOT].T for n in range(4)
        )
        content_grad, place_bias_grad = head_rows[0, :SLOT], head_rows[0, SLOT : 2 * SLOT]
        gain_grad, bias_grad = vectors[0], vectors[1]
    return (
        mixed,
        input_grad,
        gain_grad,
        bias_grad,
        query_grad,
        key_grad,
        value_grad,
        place_grad,
        content_grad,
        place_bias_grad,
        output_grad,
        rows[1],
        rows[2],
        inner_grad,
        rows[0],
        outer_grad,
        rows[3],
        rows[4],
    )


def solution(mesh):
    return jax.shard_map(
        local,
        mesh=mesh,
        in_specs=(
            P(("dp", "mp"), None),
            P("dp", "mp", None),
            P(("dp", "mp"), None),
            P("dp", None),
            P(("dp", "mp"), None),
            P(("dp", "mp")),
            P(("dp", "mp"), None),
            P("dp"),
            P("dp"),
            P(),
            P(),
            P(None, "mp"),
            P(None, "mp"),
            P(None, "mp"),
            P(None, "mp"),
            P("mp"),
            P("mp"),
            P("mp", None),
            P(),
            P(),
            P(None, "mp"),
            P("mp"),
            P("mp", None),
            P(),
            P(),
        ),
        out_specs=(
            P(("dp", "mp"), None),
            P(("dp", "mp"), None),
            P(),
            P(),
            P(None, "mp"),
            P(None, "mp"),
            P(None, "mp"),
            P(None, "mp"),
            P("mp"),
            P("mp"),
            P("mp", None),
            P(),
            P(),
            P(None, "mp"),
            P("mp"),
            P("mp", None),
            P(),
            P(),
        ),
        check_vma=False,
    )
```

```python
import math

import jax
import jax.numpy as jnp
import numpy as np
from jax import lax
from jax.experimental import pallas as pl
from jax.experimental.pallas import tpu as pltpu
from jax.sharding import PartitionSpec as P

D = 512
HD = 64
SEG = 512
MEM = 512
KEYS = 1024
SLOT = 128
EPS = 1e-05
F32 = jnp.float32
BF16 = jnp.bfloat16
GELU_C = math.sqrt(2.0 / math.pi)
SCALE = HD ** (-0.5)
VMEM = pl.BlockSpec(memory_space=pltpu.VMEM)
SMEM = pl.BlockSpec(memory_space=pltpu.SMEM)
ANY = pl.BlockSpec(memory_space=pl.ANY)


def position_table():
    distance = (KEYS - 1 - np.arange(KEYS)).astype(np.float32)
    exponent = np.arange(0, D, 2).astype(np.float32) / np.float32(D)
    angles = distance[:, None] * np.exp(np.float32(-math.log(10000.0)) * exponent)[None, :]
    table = np.concatenate([np.sin(angles), np.cos(angles)], axis=1).astype(np.float32)
    return jnp.asarray(table).astype(BF16)


def call(body, outs, ins, us=1, scratch=(), smem=0, after=(), vmem=56, late=(), early=()):
    count, given = len(ins), len(scratch)

    def run(*refs):
        in_refs = list(refs[:count])
        out_refs = list(refs[count + len(after) :][: len(outs)])
        rest = refs[count + len(after) + len(outs) :]
        own, rest = rest[:given], rest[given:]
        if not late and not early:
            body(*in_refs, *out_refs, *own)
            return
        sems = rest[-1]
        arriving, leaving = [], {}
        for k, n in enumerate(late):
            arriving.append(pltpu.make_async_copy(in_refs[n], rest[k], sems.at[k]))
            arriving[-1].start()
            in_refs[n] = rest[k]
        for k, n in enumerate(early):
            near = rest[len(late) + k]
            leaving[n] = pltpu.make_async_copy(near, out_refs[n], sems.at[len(late) + k])
            out_refs[n] = near

        def arrive():
            for copy in arriving:
                copy.wait()

        body(arrive, lambda n: leaving[n].start(), *in_refs, *out_refs, *own)
        for copy in leaving.values():
            copy.wait()

    extra = [pltpu.VMEM(ins[n].shape, ins[n].dtype) for n in late]
    extra += [pltpu.VMEM(outs[n].shape, outs[n].dtype) for n in early]
    if extra:
        extra.append(pltpu.SemaphoreType.DMA((len(extra),)))
    nbytes = sum(a.size * a.dtype.itemsize for a in ins)
    return pl.pallas_call(
        run,
        out_shape=outs,
        in_specs=[SMEM] * smem
        + [ANY if n in late else VMEM for n in range(smem, count)]
        + [ANY] * len(after),
        out_specs=tuple(ANY if n in early else VMEM for n in range(len(outs))),
        scratch_shapes=list(scratch) + extra,
        compiler_params=pltpu.CompilerParams(vmem_limit_bytes=vmem * 2**20),
        cost_estimate=pl.CostEstimate(flops=us * 10**9, bytes_accessed=nbytes, transcendentals=0),
    )(*ins, *after)


def shape(dims, dtype):
    return jax.ShapeDtypeStruct(dims, dtype)


def mm(a, b):
    return jnp.dot(a, b, preferred_element_type=F32)


def mm_nt(a, b):
    return lax.dot_general(a, b, (((1,), (1,)), ((), ())), preferred_element_type=F32)


def mm_tn(a, b):
    return lax.dot_general(a, b, (((0,), (0,)), ((), ())), preferred_element_type=F32)


def mm_tt(a, b):
    return lax.dot_general(a, b, (((0,), (1,)), ((), ())), preferred_element_type=F32)


def norm_parts(values):
    average = jnp.mean(values, axis=-1, keepdims=True)
    centred = values - average
    spread = jnp.mean(centred * centred, axis=-1, keepdims=True)
    inverse = lax.rsqrt(spread + EPS)
    return centred * inverse, inverse


def norm_back(grad, gain, xhat, inverse):
    scaled = grad * gain
    return inverse * (
        scaled
        - jnp.mean(scaled, axis=-1, keepdims=True)
        - xhat * jnp.mean(scaled * xhat, axis=-1, keepdims=True)
    )


def head_lanes(rows, h):
    lane = lax.broadcasted_iota(jnp.int32, (rows, SLOT), 1)
    return (lane // HD) == h


def of_head(values, h):
    return jnp.where(head_lanes(values.shape[0], h), values, jnp.zeros_like(values))


HEAD_PACK = D + 16
FEED_PACK = 2 * D + SLOT


def query_of(pack):
    return pack[0:D, 0:SLOT]


def key_value_of(pack):
    return pack[0:D, SLOT : 3 * SLOT]


def place_of(pack):
    return pack[0:D, 3 * SLOT : 4 * SLOT]


def start_kernel(
    place_ref, mem_ref, wq, wk, wv, wp, ib_ref, cb_ref, pb_ref,
    m0, m1, m2, m3, pack_ref,
):
    me = place_ref[0]
    for k, block in enumerate((m0, m1, m2, m3)):
        block[...] = mem_ref[me ^ k]
    for n, w in enumerate((wq, wk, wv, wp)):
        pack_ref[0:D, n * SLOT : (n + 1) * SLOT] = w[...]
    biases = jnp.concatenate([cb_ref[...], pb_ref[...]] * 2, axis=1)
    high = biases.astype(BF16).astype(F32)
    middle = (biases - high).astype(BF16).astype(F32)
    rows = jnp.concatenate(
        [ib_ref[...].astype(F32), high, middle, biases - high - middle, jnp.zeros((12, D), F32)],
        axis=0,
    )
    pack_ref[D:, :] = rows.astype(BF16)


def feed_pack_kernel(wi, wu, wo, pack_ref):
    pack_ref[0:D, :] = wi[...]
    pack_ref[D : 2 * D, :] = wu[...]
    pack_ref[2 * D :, :] = wo[...]


def normed_rows(me, m0, m1, m2, m3, x_ref, g_ref, b_ref, keys_ref):
    gain, offset = g_ref[...], b_ref[...]
    for k, block in enumerate((m0, m1, m2, m3)):
        xhat, _ = norm_parts(block[...].astype(F32))
        start = pl.multiple_of((me ^ k) * SLOT, SLOT)
        keys_ref[pl.ds(start, SLOT), :] = (xhat * gain + offset).astype(BF16)
    xhat, _ = norm_parts(x_ref[...].astype(F32))
    keys_ref[MEM:, :] = (xhat * gain + offset).astype(BF16)


def first_attend_kernel(
    arrive, send, place_ref, mem_ref, doc_ref, m0, m1, m2, m3, x_ref, g_ref, b_ref, table_ref,
    h0, h1, *refs,
):
    *out_refs, keys_ref, bias_ref = refs
    normed_rows(place_ref[0], m0, m1, m2, m3, x_ref, g_ref, b_ref, keys_ref)
    send(16)
    attend_kernel(
        arrive, send, place_ref, mem_ref, doc_ref, keys_ref, table_ref, h0, h1, *out_refs, bias_ref
    )


def attend_kernel(
    arrive, send, place_ref, mem_ref, doc_ref, keys_ref, table_ref, h0, h1, *refs
):
    out_refs, ib_refs, bias_ref = refs[:14], refs[14:16], refs[16]
    me = place_ref[0]
    low = MEM - mem_ref[me]
    high = MEM + doc_ref[me]
    place_k = lax.broadcasted_iota(jnp.int32, (SEG, KEYS), 1)
    place_q = lax.broadcasted_iota(jnp.int32, (SEG, KEYS), 0)
    live = (place_k >= low) & (place_k <= MEM + place_q) & (place_k < high)
    bias_ref[...] = jnp.where(live, 0.0, -1e30)
    arrive()
    for s, pack in enumerate((h0, h1)):
        probs_ref, qc_ref, qp_ref, kr_ref, vr_ref, pk_ref, att_ref = out_refs[7 * s : 7 * s + 7]
        small = pack[D:, :].astype(F32)
        ib_refs[s][...] = small[0:1]
        offsets = small[1:2] + small[2:3] + small[3:4]
        query = mm(keys_ref[MEM:, :], query_of(pack))
        qc_ref[...] = (query + offsets[:, :SLOT]).astype(BF16)
        qp_ref[...] = (query + offsets[:, SLOT : 2 * SLOT]).astype(BF16)
        both = mm(keys_ref[...], key_value_of(pack)).astype(BF16)
        kr_ref[...] = both[:, :SLOT]
        vr_ref[...] = both[:, SLOT:]
        pk_ref[...] = mm(table_ref[...], place_of(pack)).astype(BF16)
        parts = []
        for h in range(2):
            content = mm_nt(of_head(qc_ref[...], h), kr_ref[...])
            place = mm_nt(of_head(qp_ref[...], h), pk_ref[...])
            place = pltpu.roll(place, KEYS - SEG + 1, 1, stride=1, stride_axis=0)
            scores = (content + place) * SCALE + bias_ref[...]
            largest = jnp.max(scores, axis=-1, keepdims=True)
            raised = jnp.exp(scores - largest)
            total = jnp.sum(raised, axis=-1, keepdims=True)
            probs = (raised * (1.0 / total)).astype(BF16)
            probs_ref[h] = probs
            parts.append(mm(probs, vr_ref[...]))
        att_ref[...] = jnp.where(head_lanes(SEG, 0), parts[0], parts[1]).astype(BF16)
        for n in range(7):
            send(7 * s + n)


def feed_kernel(
    arrive, send,
    x_ref, t0, t1, t2, t3, g_ref, b_ref, h0, h1, h2, h3, f0, f1, f2, f3, ob_ref,
    middle_ref, hidden_ref, nm_ref, act_ref, slope_ref,
):
    middle = x_ref[...].astype(F32)
    packs = (f0, f1, f2, f3)
    for att, pack in zip((t0, t1, t2, t3), packs):
        middle = middle + mm(att[...], pack[2 * D :, :])
    middle_ref[...] = middle
    send(0)
    xhat, _ = norm_parts(middle)
    normed = (xhat * g_ref[...] + b_ref[...]).astype(BF16)
    nm_ref[...] = normed
    send(2)
    hidden = middle + ob_ref[...]
    for s, (small, pack) in enumerate(zip((h0, h1, h2, h3), packs)):
        pre = mm(normed, pack[0:D, :]) + small[...]
        square = pre * pre
        bend = jnp.tanh(GELU_C * (pre + 0.044715 * (pre * square)))
        act = (0.5 * pre * (1.0 + bend)).astype(BF16)
        slope = 0.5 * (1.0 + bend) + (0.5 * GELU_C) * pre * (1.0 - bend * bend) * (
            1.0 + (3 * 0.044715) * square
        )
        act_ref[s] = act
        slope_ref[s] = slope.astype(BF16)
        hidden = hidden + mm(act, pack[D : 2 * D, :])
    send(3)
    send(4)
    hidden_ref[...] = hidden


FEED_ROWS = D + SLOT + 16


def mix_kernel(
    arrive, send,
    place_ref, doc_ref, fetched, slots_ref, cot_ref, hidden_ref, gate_ref, g_ref,
    middle_ref, nm_ref, act_ref, slope_ref, t0, t1, t2, t3, f0, f1, f2, f3,
    mixed_ref, outer_keep, outer_send, gm_ref, a0, a1, a2, a3, inner_keep, inner_send,
    gh_ref, pre_ref,
):
    total = fetched.shape[0]
    docs = doc_ref[place_ref[0]]
    gate = gate_ref[...]
    scale = 1.0 / math.sqrt(D)
    step = 128
    gate_grad = jnp.zeros((1, D), F32)
    for c in range(SEG // step):
        span = slice(c * step, (c + 1) * step)
        lane = lax.broadcasted_iota(jnp.int32, (step, total), 1)
        near = []
        for j in range(4):
            pick = jnp.where(slots_ref[span, j : j + 1] == lane, 1.0, 0.0).astype(BF16)
            near.append(mm(pick, fetched[...]))
        hidden = hidden_ref[span, :]
        token = c * step + lax.broadcasted_iota(jnp.int32, (step, 1), 0)
        grad_mixed = cot_ref[span, :].astype(F32) * jnp.where(token < docs, 1.0, 0.0)
        rel = [jnp.sum(hidden * n, axis=-1, keepdims=True) * scale for n in near]
        top = jnp.maximum(jnp.maximum(rel[0], rel[1]), jnp.maximum(rel[2], rel[3]))
        raised = [jnp.exp(r - top) for r in rel]
        inverse = 1.0 / (raised[0] + raised[1] + raised[2] + raised[3])
        alpha = [r * inverse for r in raised]
        recalled = sum(a * n for a, n in zip(alpha, near))
        logit = jnp.sum(hidden * gate, axis=-1, keepdims=True)
        gating = jax.nn.sigmoid(logit)
        apart = recalled - hidden
        mixed_ref[span, :] = (hidden + gating * apart).astype(BF16)
        grad_recalled = gating * grad_mixed
        grad_gating = jnp.sum(grad_mixed * apart, axis=-1, keepdims=True)
        grad_logit = grad_gating * gating * (1.0 - gating)
        grad_alpha = [jnp.sum(grad_recalled * n, axis=-1, keepdims=True) for n in near]
        weighed = sum(a * g for a, g in zip(alpha, grad_alpha))
        grad_rel = [a * (g - weighed) * scale for a, g in zip(alpha, grad_alpha)]
        grad_hidden = grad_mixed - grad_recalled + grad_logit * gate
        grad_hidden = grad_hidden + sum(g * n for g, n in zip(grad_rel, near))
        gh_ref[span, :] = grad_hidden
        gate_grad = gate_grad + jnp.sum(grad_logit * hidden, axis=0, keepdims=True)
    send(0)
    arrive()
    low = gh_ref[...].astype(BF16)
    low_t = low.T
    for s, pack in enumerate((f0, f1, f2, f3)):
        grad_act = mm_nt(low, pack[D : 2 * D, :])
        pre_ref[s] = (grad_act * slope_ref[s].astype(F32)).astype(BF16)
        (outer_send if s % 2 else outer_keep)[s // 2] = mm(low_t, act_ref[s]).astype(BF16)
    send(1)
    send(2)
    grad_hidden = gh_ref[...]
    normed_t = nm_ref[...].T
    packs = (f0, f1, f2, f3)
    outer_bias_grad = jnp.sum(grad_hidden, axis=0, keepdims=True)
    grad_nm = jnp.zeros((SEG, D), F32)
    for s, pack in enumerate(packs):
        pay = inner_send if s % 2 else inner_keep
        pay[s // 2, 0:D, :] = mm(normed_t, pre_ref[s]).astype(BF16)
        grad_nm = grad_nm + mm_nt(pre_ref[s], pack[0:D, :])
    xhat, inverse = norm_parts(middle_ref[...])
    gain_grad = jnp.sum(grad_nm * xhat, axis=0, keepdims=True)
    bias_grad = jnp.sum(grad_nm, axis=0, keepdims=True)
    grad_middle = grad_hidden + norm_back(grad_nm, g_ref[...], xhat, inverse)
    gm_ref[...] = grad_middle
    middle_low = grad_middle.astype(BF16)
    zeros = jnp.zeros((11, D), F32)
    for s, (att, grad_att, pack) in enumerate(
        zip((t0, t1, t2, t3), (a0, a1, a2, a3), packs)
    ):
        pay = inner_send if s % 2 else inner_keep
        pay[s // 2, D : D + SLOT, :] = mm_tn(att[...], middle_low).astype(BF16)
        grad_att[...] = mm_nt(middle_low, pack[2 * D :, :]).astype(BF16)
        inner_bias_grad = jnp.sum(pre_ref[s].astype(F32), axis=0, keepdims=True)
        rows = jnp.concatenate(
            [inner_bias_grad, gain_grad, bias_grad, outer_bias_grad, gate_grad, zeros],
            axis=0,
        )
        pay[s // 2, D + SLOT :, :] = rows.astype(BF16)


HEAD_ROWS = 4 * SLOT + 16


def attend_back_kernel(
    keys_ref, table_ref, probs_ref, qc_ref, qp_ref, kr_ref, vr_ref, pk_ref, ga_ref,
    pay_ref, both_ref, gq_ref,
):
    half = SEG // 2
    across = lax.broadcasted_iota(jnp.int32, (half, half), 1)
    down = lax.broadcasted_iota(jnp.int32, (half, half), 0)
    swap = jnp.where(across + down == half - 1, 1.0, 0.0).astype(BF16)

    def flip(values):
        return jnp.concatenate([mm(swap, values[half:]), mm(swap, values[:half])], axis=0)

    keys_in = keys_ref[...]
    normed = keys_ref[MEM:, :]
    grad_v = jnp.zeros((SLOT, KEYS), F32)
    grad_k = jnp.zeros((SLOT, KEYS), F32)
    grad_p = jnp.zeros((SLOT, KEYS), F32)
    grad_c = jnp.zeros((SEG, SLOT), F32)
    grad_place = jnp.zeros((SEG, SLOT), F32)
    qp_flip = flip(qp_ref[...]).astype(BF16)
    for h in range(2):
        probs = probs_ref[h]
        grad_out = of_head(ga_ref[...], h)
        grad_probs = mm_nt(grad_out, vr_ref[...])
        wide = probs.astype(F32)
        weighed = jnp.sum(wide * grad_probs, axis=-1, keepdims=True)
        grad_scores = (wide * (grad_probs - weighed)).astype(BF16)
        grad_v = grad_v + mm_tn(grad_out, probs)
        grad_k = grad_k + mm_tn(of_head(qc_ref[...], h), grad_scores)
        grad_c = grad_c + mm(grad_scores, of_head(kr_ref[...], h))
        turned = pltpu.roll(flip(grad_scores), 0, 1, stride=1, stride_axis=0).astype(BF16)
        grad_place = grad_place + mm(turned, of_head(pk_ref[...], h))
        grad_p = grad_p + mm_tn(of_head(qp_flip, h), turned)
    grad_v = grad_v.astype(BF16)
    grad_k = (grad_k * SCALE).astype(BF16)
    grad_p = (grad_p * SCALE).astype(BF16)
    grad_c = grad_c * SCALE
    grad_place = grad_place * SCALE
    high = grad_place.astype(BF16)
    rest = (grad_place - high.astype(F32)).astype(BF16)
    grad_q = (grad_c + flip(high) + flip(rest)).astype(BF16)
    gq_ref[...] = grad_q
    both_ref[0:SLOT, :] = grad_k
    both_ref[SLOT:, :] = grad_v
    pay_ref[0:SLOT, :] = mm_tn(grad_q, normed).astype(BF16)
    pay_ref[SLOT : 3 * SLOT, :] = mm(both_ref[...], keys_in).astype(BF16)
    pay_ref[3 * SLOT : 4 * SLOT, :] = mm(grad_p, table_ref[...]).astype(BF16)
    biases = jnp.concatenate(
        [
            jnp.sum(grad_c, axis=0, keepdims=True),
            jnp.sum(grad_place, axis=0, keepdims=True),
            jnp.zeros((1, D - 2 * SLOT), F32),
        ],
        axis=1,
    )
    pay_ref[4 * SLOT :, :] = jnp.concatenate([biases, jnp.zeros((15, D), F32)], axis=0).astype(
        BF16
    )


def input_kernel(
    place_ref, x_ref, m0, m1, m2, m3, gm_ref, g_ref, both_0, both_1, both_2, both_3,
    gq_0, gq_1, gq_2, gq_3, h0, h1, h2, h3,
    grad_ref, vectors_ref,
    total_ref,
):
    me = place_ref[0]
    packs = (h0, h1, h2, h3)
    total = jnp.zeros((KEYS, D), F32)
    for both, pack in zip((both_0, both_1, both_2, both_3), packs):
        total = total + mm_tt(both[...], key_value_of(pack))
    total_ref[...] = total
    grad = total_ref[MEM:, :]
    for gq, pack in zip((gq_0, gq_1, gq_2, gq_3), packs):
        grad = grad + mm_nt(gq[...], query_of(pack))
    xhat, inverse = norm_parts(x_ref[...].astype(F32))
    grad_ref[...] = gm_ref[...] + norm_back(grad, g_ref[...], xhat, inverse)
    gain_grad = jnp.sum(grad * xhat, axis=0, keepdims=True)
    bias_grad = jnp.sum(grad, axis=0, keepdims=True) + jnp.sum(
        total_ref[:MEM, :], axis=0, keepdims=True
    )
    for k, block in enumerate((m0, m1, m2, m3)):
        seen, _ = norm_parts(block[...].astype(F32))
        start = pl.multiple_of((me ^ k) * SLOT, SLOT)
        gain_grad = gain_grad + jnp.sum(
            total_ref[pl.ds(start, SLOT), :] * seen, axis=0, keepdims=True
        )
    vectors_ref[...] = jnp.concatenate([gain_grad, bias_grad, jnp.zeros((6, D), F32)], axis=0)


def swap_with(values, axis, k):
    n = lax.axis_size(axis)
    return lax.ppermute(values, axis, [(i, i ^ k) for i in range(n)])


def turn(values, axis):
    return lax.all_to_all(values, axis, split_axis=0, concat_axis=0, tiled=True)


def by_steps():
    return lax.axis_size("dp") == 8


def when(values, after):
    return lax.optimization_barrier((values, after))[0]


def wide(*terms):
    return sum(t.astype(F32) for t in terms)


def part_of(values, index, count):
    size = values.shape[0] // count
    return lax.dynamic_slice_in_dim(values, index * size, size)


def in_order(place_ref, own, other, half):
    first = place_ref[1] == 0
    top = jnp.where(first, own[:half, :], other[:half, :])
    bottom = jnp.where(first, other[:half, :], own[:half, :])
    vectors = None
    if own.shape[0] > half:
        vectors = own[half:, :].astype(F32) + other[half:, :].astype(F32)
    return top, bottom, vectors


def outer_out_kernel(place_ref, own, other, out_ref):
    top, bottom, _ = in_order(place_ref, own, other, D // 2)
    out_ref[...] = jnp.concatenate([top, bottom], axis=0).T.astype(F32)


def inner_out_kernel(place_ref, own, other, inner_ref, output_ref, *rows_refs):
    half = (D + SLOT) // 2
    top, bottom, vectors = in_order(place_ref, own, other, half)
    inner_ref[0:half, :] = top.astype(F32)
    inner_ref[half:, :] = bottom[: D - half].astype(F32)
    output_ref[...] = bottom[D - half :].astype(F32)
    for n, ref in enumerate(rows_refs):
        ref[...] = vectors[n : n + 1]


def head_out_kernel(place_ref, own, other, q_ref, k_ref, v_ref, p_ref, *rows_refs):
    top, bottom, vectors = in_order(place_ref, own, other, D // 2)
    full = jnp.concatenate([top, bottom], axis=0)
    for n, ref in enumerate((q_ref, k_ref, v_ref, p_ref)):
        ref[...] = full[n * SLOT : (n + 1) * SLOT].T.astype(F32)
    content, place, gain, bias = rows_refs
    content[...] = vectors[0:1, :SLOT]
    place[...] = vectors[0:1, SLOT : 2 * SLOT]
    gain[...] = vectors[1:2]
    bias[...] = vectors[2:3]


class Summed:
    def __init__(self, place, rows, tail):
        self.place, self.rows, self.tail = place, rows, tail
        self.level = 0
        self.vectors = None

    def send_half(self, terms):
        bit = self.place[1 + self.level]
        self.kept = [part_of(t, bit, 2) for t in terms]
        sent = wide(*(part_of(t, 1 - bit, 2) for t in terms)).astype(BF16)
        self.got = swap_with(sent, "dp", 2**self.level)
        self.level += 1
        return sent

    def first(self, terms, after):
        terms = when(terms, after)
        if self.tail:
            self.vectors = wide(*(t[self.rows :] for t in terms)).astype(BF16)
        return self.send_half([t[: self.rows] for t in terms])

    def down(self, after):
        return self.send_half([*self.kept, when(self.got, after)])

    def send_back(self, part):
        self.level -= 1
        self.part = part
        message = part if self.vectors is None else jnp.concatenate([part, self.vectors], axis=0)
        self.got = swap_with(message, "dp", 2**self.level)
        return message

    def turn(self, after, vec=()):
        part = wide(*self.kept, when(self.got, after)).astype(BF16)
        if vec:
            lines = wide(*vec)[0:2].astype(BF16)
            self.vectors = jnp.concatenate([self.vectors[0:1], lines, self.vectors[3:]], axis=0)
        return self.send_back(part)

    def cross(self, after):
        part = wide(*self.kept, when(self.got, after)).astype(BF16)
        rows = part.shape[0] // 2
        self.kept, self.got = part[:rows], swap_with(part[rows:], "mp", 2)
        return part

    def turn_near(self, after):
        return self.send_back(wide(self.kept, when(self.got, after)).astype(BF16))

    def joined(self, got):
        rows = self.part.shape[0]
        low = self.place[1 + self.level] == 0
        other = got[:rows]
        if self.vectors is not None:
            self.vectors = wide(self.vectors, got[rows:]).astype(BF16)
        return jnp.concatenate(
            [jnp.where(low, self.part, other), jnp.where(low, other, self.part)], axis=0
        )

    def up(self, after):
        return self.send_back(self.joined(when(self.got, after)))

    def out(self, kernel, outs, after):
        own = self.part
        if self.vectors is not None:
            own = jnp.concatenate([own, self.vectors], axis=0)
        return call(kernel, outs, [self.place, own, self.got], smem=1, after=after)


def dp_sum(values):
    n = lax.axis_size("dp")
    rows = values.shape[0]
    got = turn(values.reshape(n, rows // n, D), "dp")
    part = jnp.sum(got.astype(F32), axis=0).astype(BF16)
    return turn(jnp.broadcast_to(part[None], (n,) + part.shape), "dp").reshape(rows, D)


def dp_vectors(values):
    n = lax.axis_size("dp")
    return jnp.sum(turn(jnp.broadcast_to(values[None], (n,) + values.shape), "dp"), axis=0)


def all_shards(values):
    one = swap_with(values, "mp", 1)
    two = swap_with(values, "mp", 2)
    three = swap_with(two, "mp", 1)
    return [values, one, two, three]


def local(
    block_input,
    memory,
    cotangent,
    neighbour_table,
    requests,
    counts,
    neighbour_slots,
    memory_lengths,
    document_lengths,
    first_gain,
    first_bias,
    query_weight,
    key_weight,
    value_weight,
    position_weight,
    content_bias,
    position_bias,
    output_weight,
    second_gain,
    second_bias,
    inner_weight,
    inner_bias,
    outer_weight,
    outer_bias,
    gate_weight,
):
    data_index = lax.axis_index("dp").astype(jnp.int32)
    place = jnp.stack(
        [lax.axis_index("mp").astype(jnp.int32)] + [data_index // 2**n % 2 for n in range(3)]
    )
    data_size = lax.axis_size("dp")
    capacity = requests.shape[1]
    row = lambda v: v.reshape(1, -1)
    g1, b1, g2, b2 = row(first_gain), row(first_bias), row(second_gain), row(second_bias)
    low_square = shape((SEG, D), BF16)
    block = shape((SLOT, D), BF16)

    wanted = turn(requests, "dp").reshape(requests.shape)

    *mem_own, head_pack = call(
        start_kernel,
        (block, block, block, block, shape((HEAD_PACK, D), BF16)),
        [
            place, memory, query_weight, key_weight, value_weight, position_weight,
            row(inner_bias), row(content_bias), row(position_bias),
        ],
        smem=1,
    )
    mem = [mem_own[0]] + [swap_with(mem_own[k], "mp", k) for k in (1, 2, 3)]
    heads = all_shards(head_pack)
    found = jnp.take(neighbour_table, wanted, axis=0, mode="clip")
    fetched = turn(found, "dp").reshape(data_size * capacity, D)
    (feed_pack,) = call(
        feed_pack_kernel,
        (shape((FEED_PACK, D), BF16),),
        [inner_weight, outer_weight, output_weight],
        after=[found],
    )
    feeds = all_shards(feed_pack)[:3]
    table = position_table()

    slot = lambda rows: shape((rows, SLOT), BF16)
    line = shape((1, D), F32)
    of_slot = (
        shape((2, SEG, KEYS), BF16),
        slot(SEG), slot(SEG), slot(KEYS), slot(KEYS), slot(KEYS), slot(SEG),
    )
    *results_a, keys_in = call(
        first_attend_kernel,
        of_slot * 2 + (line,) * 2 + (shape((KEYS, D), BF16),),
        [
            place, memory_lengths, document_lengths, *mem, block_input, g1, b1, table, *heads[:2],
        ],
        scratch=[pltpu.VMEM((SEG, KEYS), F32)],
        smem=3,
        after=[feed_pack],
        us=20,
        late=range(10, 13),
        early=(*range(14), 16),
    )
    results_b = call(
        attend_kernel,
        of_slot * 2 + (line,) * 2,
        [place, memory_lengths, document_lengths, keys_in, table, *heads[2:]],
        scratch=[pltpu.VMEM((SEG, KEYS), F32)],
        smem=3,
        us=20,
        early=range(14),
    )
    feeds.append(swap_with(when(feeds[2], results_b[0]), "mp", 1))
    saved = [r[7 * n : 7 * n + 7] for r in (results_a, results_b) for n in range(2)]
    inner_biases = [*results_a[14:16], *results_b[14:16]]
    attended = [v[-1] for v in saved]

    square = shape((SEG, D), F32)
    units = shape((4, SEG, D), BF16)
    middle, hidden, normed_middle, activation, slope = call(
        feed_kernel,
        (square, square, low_square, units, units),
        [block_input, *attended, g2, b2, *inner_biases, *feeds, row(outer_bias)],
        us=10,
        early=(0, 2, 3, 4),
    )

    pair = shape((2, D, D), BF16)
    slot_grad = shape((SEG, SLOT), BF16)
    inner_pair = shape((2, FEED_ROWS, D), BF16)
    mixed, outer_keep, outer_send, grad_middle, *grad_att, inner_keep, inner_send = call(
        mix_kernel,
        (low_square, pair, pair, square, *[slot_grad] * 4, inner_pair, inner_pair),
        [
            place, document_lengths, fetched, neighbour_slots, cotangent, hidden,
            row(gate_weight), g2, middle, normed_middle, activation, slope, *attended, *feeds,
        ],
        scratch=[pltpu.VMEM((SEG, D), F32), pltpu.VMEM((4, SEG, D), BF16)],
        smem=2,
        us=20,
        vmem=56,
        late=range(8, 20),
        early=(0, 1, 2),
    )

    def attend_back(n, after):
        return call(
            attend_back_kernel,
            (shape((HEAD_ROWS, D), BF16), shape((2 * SLOT, KEYS), BF16), shape((SEG, SLOT), BF16)),
            [keys_in, table, *saved[n][:-1], grad_att[n]],
            us=9,
            after=after,
            vmem=24,
        )

    def two(keep, send, after):
        keep, got = when((keep, swap_with(send, "mp", 1)), after)
        near, far = (wide(keep[n], got[n]).astype(BF16) for n in range(2))
        return near, swap_with(far, "mp", 2)

    steps = by_steps()
    outer = Summed(place, 2 * D, 0)
    keep, got = when((outer_keep, swap_with(outer_send, "mp", 1)), grad_middle)
    if steps:
        both = wide(keep, got).reshape(2, 8, D // 8, D).swapaxes(0, 1).reshape(2 * D, D).astype(BF16)
        at = outer.first([both], [grad_middle])
    else:
        at = outer_near = wide(keep[0], got[0]).astype(BF16)
        outer_far = swap_with(wide(keep[1], got[1]).astype(BF16), "mp", 2)
    pay_3, both_3, gq_3 = attend_back(3, [at])
    inner_near, inner_far = two(inner_keep, inner_send, [gq_3])
    pay_2, both_2, gq_2 = attend_back(2, [inner_near])
    head_far = wide(*when((pay_2, swap_with(pay_3, "mp", 1)), gq_2)).astype(BF16)
    head_got = swap_with(head_far, "mp", 2)
    inner, head = Summed(place, D + SLOT, 1), Summed(place, D, 1)
    eight = shape((8, D), F32)

    def input_back(after):
        return call(
            input_kernel,
            (square, eight),
            [
                place, block_input, *mem, grad_middle, g1, both_0, both_1, both_2, both_3,
                gq_0, gq_1, gq_2, gq_3, *heads,
            ],
            scratch=[pltpu.VMEM((KEYS, D), F32)],
            smem=1,
            after=after,
            us=6,
            vmem=24,
        )

    weight = shape((D, SLOT), F32)
    short = shape((1, SLOT), F32)
    head_outs = (weight,) * 4 + (short, short, line, line)
    inner_outs = (square, shape((SLOT, D), F32)) + (line,) * 5
    if steps:
        at = outer.down([head_far])
        pay_1, both_1, gq_1 = attend_back(1, [at])
        at = outer.down([gq_1])
        pay_0, both_0, gq_0 = attend_back(0, [at])
        at = inner.first([inner_near, inner_far], [gq_0])
        input_grad, vectors = input_back([at])
        at = outer.cross([vectors])
        at = head.first([pay_0, swap_with(pay_1, "mp", 1), head_got], [at])
        at = inner.down([at])
        at = outer.turn_near([at])
        at = head.down([at])
        at = inner.down([at])
        vectors = wide(*when((vectors, swap_with(vectors, "mp", 1)), at))
        at = outer.up([vectors])
        at = head.down([at])
        at = inner.turn([at])
        at = outer.up([at])
        at = head.turn([at], [vectors, swap_with(vectors, "mp", 2)])
        at = inner.up([at])
        at = head.up([at])
        (outer_grad,) = outer.out(outer_out_kernel, (square,), [at])
        at = inner.up([outer_grad])
        at = head.up([at])
        inner_grad, output_grad, *rows = inner.out(inner_out_kernel, inner_outs, [at])
        query_grad, key_grad, value_grad, place_grad, *head_rows = head.out(
            head_out_kernel, head_outs, [inner_grad]
        )
        content_grad, place_bias_grad, gain_grad, bias_grad = (v[0] for v in head_rows)
        rows = [v[0] for v in rows]
    else:
        pay_1, both_1, gq_1 = attend_back(1, [head_far])
        pay_0, both_0, gq_0 = attend_back(0, [gq_1])
        outer = wide(outer_near, outer_far)
        inner = wide(inner_near, inner_far)
        head = wide(pay_0, swap_with(pay_1, "mp", 1), head_got)
        input_grad, vectors = input_back([gq_0])
        vectors = vectors + swap_with(vectors, "mp", 1)
        vectors = dp_vectors(vectors + swap_with(vectors, "mp", 2))
        outer_grad = dp_sum(outer.astype(BF16)).astype(F32).T
        inner_grad = dp_sum(inner[: D + SLOT].astype(BF16)).astype(F32)
        rows = dp_vectors(inner[D + SLOT :])
        inner_grad, output_grad = inner_grad[:D], inner_grad[D:]
        head_rows = dp_vectors(head[4 * SLOT :])
        grads = dp_sum(head[: 4 * SLOT].astype(BF16)).astype(F32)
        query_grad, key_grad, value_grad, place_grad = (
            grads[n * SLOT : (n + 1) * SLOT].T for n in range(4)
        )
        content_grad, place_bias_grad = head_rows[0, :SLOT], head_rows[0, SLOT : 2 * SLOT]
        gain_grad, bias_grad = vectors[0], vectors[1]
    return (
        mixed,
        input_grad,
        gain_grad,
        bias_grad,
        query_grad,
        key_grad,
        value_grad,
        place_grad,
        content_grad,
        place_bias_grad,
        output_grad,
        rows[1],
        rows[2],
        inner_grad,
        rows[0],
        outer_grad,
        rows[3],
        rows[4],
    )


def solution(mesh):
    return jax.shard_map(
        local,
        mesh=mesh,
        in_specs=(
            P(("dp", "mp"), None),
            P("dp", "mp", None),
            P(("dp", "mp"), None),
            P("dp", None),
            P(("dp", "mp"), None),
            P(("dp", "mp")),
            P(("dp", "mp"), None),
            P("dp"),
            P("dp"),
            P(),
            P(),
            P(None, "mp"),
            P(None, "mp"),
            P(None, "mp"),
            P(None, "mp"),
            P("mp"),
            P("mp"),
            P("mp", None),
            P(),
            P(),
            P(None, "mp"),
            P("mp"),
            P("mp", None),
            P(),
            P(),
        ),
        out_specs=(
            P(("dp", "mp"), None),
            P(("dp", "mp"), None),
            P(),
            P(),
            P(None, "mp"),
            P(None, "mp"),
            P(None, "mp"),
            P(None, "mp"),
            P("mp"),
            P("mp"),
            P("mp", None),
            P(),
            P(),
            P(None, "mp"),
            P("mp"),
            P("mp", None),
            P(),
            P(),
        ),
        check_vma=False,
    )
```

```python
import math

import jax
import jax.numpy as jnp
import numpy as np
from jax import lax
from jax.experimental import pallas as pl
from jax.experimental.pallas import tpu as pltpu
from jax.sharding import PartitionSpec as P

D = 512
HD = 64
SEG = 512
MEM = 512
KEYS = 1024
SLOT = 128
EPS = 1e-05
F32 = jnp.float32
BF16 = jnp.bfloat16
GELU_C = math.sqrt(2.0 / math.pi)
SCALE = HD ** (-0.5)
VMEM = pl.BlockSpec(memory_space=pltpu.VMEM)
SMEM = pl.BlockSpec(memory_space=pltpu.SMEM)
ANY = pl.BlockSpec(memory_space=pl.ANY)


def position_table():
    distance = (KEYS - 1 - np.arange(KEYS)).astype(np.float32)
    exponent = np.arange(0, D, 2).astype(np.float32) / np.float32(D)
    angles = distance[:, None] * np.exp(np.float32(-math.log(10000.0)) * exponent)[None, :]
    table = np.concatenate([np.sin(angles), np.cos(angles)], axis=1).astype(np.float32)
    return jnp.asarray(table).astype(BF16)


def call(body, outs, ins, us=1, scratch=(), smem=0, after=(), vmem=56, late=(), early=()):
    count, given = len(ins), len(scratch)

    def run(*refs):
        in_refs = list(refs[:count])
        out_refs = list(refs[count + len(after) :][: len(outs)])
        rest = refs[count + len(after) + len(outs) :]
        own, rest = rest[:given], rest[given:]
        if not late and not early:
            body(*in_refs, *out_refs, *own)
            return
        sems = rest[-1]
        arriving, leaving = [], {}
        for k, n in enumerate(late):
            arriving.append(pltpu.make_async_copy(in_refs[n], rest[k], sems.at[k]))
            arriving[-1].start()
            in_refs[n] = rest[k]
        for k, n in enumerate(early):
            near = rest[len(late) + k]
            leaving[n] = pltpu.make_async_copy(near, out_refs[n], sems.at[len(late) + k])
            out_refs[n] = near

        def arrive():
            for copy in arriving:
                copy.wait()

        body(arrive, lambda n: leaving[n].start(), *in_refs, *out_refs, *own)
        for copy in leaving.values():
            copy.wait()

    extra = [pltpu.VMEM(ins[n].shape, ins[n].dtype) for n in late]
    extra += [pltpu.VMEM(outs[n].shape, outs[n].dtype) for n in early]
    if extra:
        extra.append(pltpu.SemaphoreType.DMA((len(extra),)))
    nbytes = sum(a.size * a.dtype.itemsize for a in ins)
    return pl.pallas_call(
        run,
        out_shape=outs,
        in_specs=[SMEM] * smem
        + [ANY if n in late else VMEM for n in range(smem, count)]
        + [ANY] * len(after),
        out_specs=tuple(ANY if n in early else VMEM for n in range(len(outs))),
        scratch_shapes=list(scratch) + extra,
        compiler_params=pltpu.CompilerParams(vmem_limit_bytes=vmem * 2**20),
        cost_estimate=pl.CostEstimate(flops=us * 10**9, bytes_accessed=nbytes, transcendentals=0),
    )(*ins, *after)


def shape(dims, dtype):
    return jax.ShapeDtypeStruct(dims, dtype)


def mm(a, b):
    return jnp.dot(a, b, preferred_element_type=F32)


def mm_nt(a, b):
    return lax.dot_general(a, b, (((1,), (1,)), ((), ())), preferred_element_type=F32)


def mm_tn(a, b):
    return lax.dot_general(a, b, (((0,), (0,)), ((), ())), preferred_element_type=F32)


def mm_tt(a, b):
    return lax.dot_general(a, b, (((0,), (1,)), ((), ())), preferred_element_type=F32)


def norm_parts(values):
    average = jnp.mean(values, axis=-1, keepdims=True)
    centred = values - average
    spread = jnp.mean(centred * centred, axis=-1, keepdims=True)
    inverse = lax.rsqrt(spread + EPS)
    return centred * inverse, inverse


def norm_back(grad, gain, xhat, inverse):
    scaled = grad * gain
    return inverse * (
        scaled
        - jnp.mean(scaled, axis=-1, keepdims=True)
        - xhat * jnp.mean(scaled * xhat, axis=-1, keepdims=True)
    )


def head_lanes(rows, h):
    lane = lax.broadcasted_iota(jnp.int32, (rows, SLOT), 1)
    return (lane // HD) == h


def of_head(values, h):
    return jnp.where(head_lanes(values.shape[0], h), values, jnp.zeros_like(values))


HEAD_PACK = D + 16
FEED_PACK = 2 * D + SLOT


def query_of(pack):
    return pack[0:D, 0:SLOT]


def key_value_of(pack):
    return pack[0:D, SLOT : 3 * SLOT]


def place_of(pack):
    return pack[0:D, 3 * SLOT : 4 * SLOT]


def start_kernel(
    place_ref, mem_ref, wq, wk, wv, wp, ib_ref, cb_ref, pb_ref,
    m0, m1, m2, m3, pack_ref,
):
    me = place_ref[0]
    for k, block in enumerate((m0, m1, m2, m3)):
        block[...] = mem_ref[me ^ k]
    for n, w in enumerate((wq, wk, wv, wp)):
        pack_ref[0:D, n * SLOT : (n + 1) * SLOT] = w[...]
    biases = jnp.concatenate([cb_ref[...], pb_ref[...]] * 2, axis=1)
    high = biases.astype(BF16).astype(F32)
    middle = (biases - high).astype(BF16).astype(F32)
    rows = jnp.concatenate(
        [ib_ref[...].astype(F32), high, middle, biases - high - middle, jnp.zeros((12, D), F32)],
        axis=0,
    )
    pack_ref[D:, :] = rows.astype(BF16)


def feed_pack_kernel(wi, wu, wo, pack_ref):
    pack_ref[0:D, :] = wi[...]
    pack_ref[D : 2 * D, :] = wu[...]
    pack_ref[2 * D :, :] = wo[...]


def normed_rows(me, m0, m1, m2, m3, x_ref, g_ref, b_ref, keys_ref):
    gain, offset = g_ref[...], b_ref[...]
    for k, block in enumerate((m0, m1, m2, m3)):
        xhat, _ = norm_parts(block[...].astype(F32))
        start = pl.multiple_of((me ^ k) * SLOT, SLOT)
        keys_ref[pl.ds(start, SLOT), :] = (xhat * gain + offset).astype(BF16)
    xhat, _ = norm_parts(x_ref[...].astype(F32))
    keys_ref[MEM:, :] = (xhat * gain + offset).astype(BF16)


def first_attend_kernel(
    arrive, send, place_ref, mem_ref, doc_ref, m0, m1, m2, m3, x_ref, g_ref, b_ref, table_ref,
    h0, h1, *refs,
):
    *out_refs, keys_ref, bias_ref = refs
    normed_rows(place_ref[0], m0, m1, m2, m3, x_ref, g_ref, b_ref, keys_ref)
    send(16)
    attend_kernel(
        arrive, send, place_ref, mem_ref, doc_ref, keys_ref, table_ref, h0, h1, *out_refs, bias_ref
    )


def attend_kernel(
    arrive, send, place_ref, mem_ref, doc_ref, keys_ref, table_ref, h0, h1, *refs
):
    out_refs, ib_refs, bias_ref = refs[:14], refs[14:16], refs[16]
    me = place_ref[0]
    low = MEM - mem_ref[me]
    high = MEM + doc_ref[me]
    place_k = lax.broadcasted_iota(jnp.int32, (SEG, KEYS), 1)
    place_q = lax.broadcasted_iota(jnp.int32, (SEG, KEYS), 0)
    live = (place_k >= low) & (place_k <= MEM + place_q) & (place_k < high)
    bias_ref[...] = jnp.where(live, 0.0, -1e30)
    arrive()
    for s, pack in enumerate((h0, h1)):
        probs_ref, qc_ref, qp_ref, kr_ref, vr_ref, pk_ref, att_ref = out_refs[7 * s : 7 * s + 7]
        small = pack[D:, :].astype(F32)
        ib_refs[s][...] = small[0:1]
        offsets = small[1:2] + small[2:3] + small[3:4]
        query = mm(keys_ref[MEM:, :], query_of(pack))
        qc_ref[...] = (query + offsets[:, :SLOT]).astype(BF16)
        qp_ref[...] = (query + offsets[:, SLOT : 2 * SLOT]).astype(BF16)
        both = mm(keys_ref[...], key_value_of(pack)).astype(BF16)
        kr_ref[...] = both[:, :SLOT]
        vr_ref[...] = both[:, SLOT:]
        pk_ref[...] = mm(table_ref[...], place_of(pack)).astype(BF16)
        parts = []
        for h in range(2):
            content = mm_nt(of_head(qc_ref[...], h), kr_ref[...])
            place = mm_nt(of_head(qp_ref[...], h), pk_ref[...])
            place = pltpu.roll(place, KEYS - SEG + 1, 1, stride=1, stride_axis=0)
            scores = (content + place) * SCALE + bias_ref[...]
            largest = jnp.max(scores, axis=-1, keepdims=True)
            raised = jnp.exp(scores - largest)
            total = jnp.sum(raised, axis=-1, keepdims=True)
            probs = (raised * (1.0 / total)).astype(BF16)
            probs_ref[h] = probs
            parts.append(mm(probs, vr_ref[...]))
        att_ref[...] = jnp.where(head_lanes(SEG, 0), parts[0], parts[1]).astype(BF16)
        for n in range(7):
            send(7 * s + n)


def feed_kernel(
    arrive, send,
    x_ref, t0, t1, t2, t3, g_ref, b_ref, h0, h1, h2, h3, f0, f1, f2, f3, ob_ref,
    middle_ref, hidden_ref, nm_ref, act_ref, slope_ref,
):
    middle = x_ref[...].astype(F32)
    packs = (f0, f1, f2, f3)
    for att, pack in zip((t0, t1, t2, t3), packs):
        middle = middle + mm(att[...], pack[2 * D :, :])
    middle_ref[...] = middle
    send(0)
    xhat, _ = norm_parts(middle)
    normed = (xhat * g_ref[...] + b_ref[...]).astype(BF16)
    nm_ref[...] = normed
    send(2)
    hidden = middle + ob_ref[...]
    for s, (small, pack) in enumerate(zip((h0, h1, h2, h3), packs)):
        pre = mm(normed, pack[0:D, :]) + small[...]
        square = pre * pre
        bend = jnp.tanh(GELU_C * (pre + 0.044715 * (pre * square)))
        act = (0.5 * pre * (1.0 + bend)).astype(BF16)
        slope = 0.5 * (1.0 + bend) + (0.5 * GELU_C) * pre * (1.0 - bend * bend) * (
            1.0 + (3 * 0.044715) * square
        )
        act_ref[s] = act
        slope_ref[s] = slope.astype(BF16)
        hidden = hidden + mm(act, pack[D : 2 * D, :])
    send(3)
    send(4)
    hidden_ref[...] = hidden


FEED_ROWS = D + SLOT + 16


def mix_kernel(
    arrive, send,
    place_ref, doc_ref, fetched, slots_ref, cot_ref, hidden_ref, gate_ref, g_ref,
    middle_ref, nm_ref, act_ref, slope_ref, t0, t1, t2, t3, f0, f1, f2, f3,
    mixed_ref, outer_keep, outer_send, gm_ref, a0, a1, a2, a3, inner_keep, inner_send,
    gh_ref, pre_ref,
):
    total = fetched.shape[0]
    docs = doc_ref[place_ref[0]]
    gate = gate_ref[...]
    scale = 1.0 / math.sqrt(D)
    step = 128
    gate_grad = jnp.zeros((1, D), F32)
    for c in range(SEG // step):
        span = slice(c * step, (c + 1) * step)
        lane = lax.broadcasted_iota(jnp.int32, (step, total), 1)
        near = []
        for j in range(4):
            pick = jnp.where(slots_ref[span, j : j + 1] == lane, 1.0, 0.0).astype(BF16)
            near.append(mm(pick, fetched[...]))
        hidden = hidden_ref[span, :]
        token = c * step + lax.broadcasted_iota(jnp.int32, (step, 1), 0)
        grad_mixed = cot_ref[span, :].astype(F32) * jnp.where(token < docs, 1.0, 0.0)
        rel = [jnp.sum(hidden * n, axis=-1, keepdims=True) * scale for n in near]
        top = jnp.maximum(jnp.maximum(rel[0], rel[1]), jnp.maximum(rel[2], rel[3]))
        raised = [jnp.exp(r - top) for r in rel]
        inverse = 1.0 / (raised[0] + raised[1] + raised[2] + raised[3])
        alpha = [r * inverse for r in raised]
        recalled = sum(a * n for a, n in zip(alpha, near))
        logit = jnp.sum(hidden * gate, axis=-1, keepdims=True)
        gating = jax.nn.sigmoid(logit)
        apart = recalled - hidden
        mixed_ref[span, :] = (hidden + gating * apart).astype(BF16)
        grad_recalled = gating * grad_mixed
        grad_gating = jnp.sum(grad_mixed * apart, axis=-1, keepdims=True)
        grad_logit = grad_gating * gating * (1.0 - gating)
        grad_alpha = [jnp.sum(grad_recalled * n, axis=-1, keepdims=True) for n in near]
        weighed = sum(a * g for a, g in zip(alpha, grad_alpha))
        grad_rel = [a * (g - weighed) * scale for a, g in zip(alpha, grad_alpha)]
        grad_hidden = grad_mixed - grad_recalled + grad_logit * gate
        grad_hidden = grad_hidden + sum(g * n for g, n in zip(grad_rel, near))
        gh_ref[span, :] = grad_hidden
        gate_grad = gate_grad + jnp.sum(grad_logit * hidden, axis=0, keepdims=True)
    send(0)
    arrive()
    low = gh_ref[...].astype(BF16)
    low_t = low.T
    for s, pack in enumerate((f0, f1, f2, f3)):
        grad_act = mm_nt(low, pack[D : 2 * D, :])
        pre_ref[s] = (grad_act * slope_ref[s].astype(F32)).astype(BF16)
        (outer_send if s % 2 else outer_keep)[s // 2] = mm(low_t, act_ref[s]).astype(BF16)
    send(1)
    send(2)
    grad_hidden = gh_ref[...]
    normed_t = nm_ref[...].T
    packs = (f0, f1, f2, f3)
    outer_bias_grad = jnp.sum(grad_hidden, axis=0, keepdims=True)
    grad_nm = jnp.zeros((SEG, D), F32)
    for s, pack in enumerate(packs):
        pay = inner_send if s % 2 else inner_keep
        pay[s // 2, 0:D, :] = mm(normed_t, pre_ref[s]).astype(BF16)
        grad_nm = grad_nm + mm_nt(pre_ref[s], pack[0:D, :])
    xhat, inverse = norm_parts(middle_ref[...])
    gain_grad = jnp.sum(grad_nm * xhat, axis=0, keepdims=True)
    bias_grad = jnp.sum(grad_nm, axis=0, keepdims=True)
    grad_middle = grad_hidden + norm_back(grad_nm, g_ref[...], xhat, inverse)
    gm_ref[...] = grad_middle
    middle_low = grad_middle.astype(BF16)
    zeros = jnp.zeros((11, D), F32)
    for s, (att, grad_att, pack) in enumerate(
        zip((t0, t1, t2, t3), (a0, a1, a2, a3), packs)
    ):
        pay = inner_send if s % 2 else inner_keep
        pay[s // 2, D : D + SLOT, :] = mm_tn(att[...], middle_low).astype(BF16)
        grad_att[...] = mm_nt(middle_low, pack[2 * D :, :]).astype(BF16)
        inner_bias_grad = jnp.sum(pre_ref[s].astype(F32), axis=0, keepdims=True)
        rows = jnp.concatenate(
            [inner_bias_grad, gain_grad, bias_grad, outer_bias_grad, gate_grad, zeros],
            axis=0,
        )
        pay[s // 2, D + SLOT :, :] = rows.astype(BF16)


HEAD_ROWS = 4 * SLOT + 16


def attend_back_kernel(
    keys_ref, table_ref, probs_ref, qc_ref, qp_ref, kr_ref, vr_ref, pk_ref, ga_ref,
    pay_ref, both_ref, gq_ref,
):
    half = SEG // 2
    across = lax.broadcasted_iota(jnp.int32, (half, half), 1)
    down = lax.broadcasted_iota(jnp.int32, (half, half), 0)
    swap = jnp.where(across + down == half - 1, 1.0, 0.0).astype(BF16)

    def flip(values):
        return jnp.concatenate([mm(swap, values[half:]), mm(swap, values[:half])], axis=0)

    keys_in = keys_ref[...]
    normed = keys_ref[MEM:, :]
    grad_v = jnp.zeros((SLOT, KEYS), F32)
    grad_k = jnp.zeros((SLOT, KEYS), F32)
    grad_p = jnp.zeros((SLOT, KEYS), F32)
    grad_c = jnp.zeros((SEG, SLOT), F32)
    grad_place = jnp.zeros((SEG, SLOT), F32)
    qp_flip = flip(qp_ref[...]).astype(BF16)
    for h in range(2):
        probs = probs_ref[h]
        grad_out = of_head(ga_ref[...], h)
        grad_probs = mm_nt(grad_out, vr_ref[...])
        wide = probs.astype(F32)
        weighed = jnp.sum(wide * grad_probs, axis=-1, keepdims=True)
        grad_scores = (wide * (grad_probs - weighed)).astype(BF16)
        grad_v = grad_v + mm_tn(grad_out, probs)
        grad_k = grad_k + mm_tn(of_head(qc_ref[...], h), grad_scores)
        grad_c = grad_c + mm(grad_scores, of_head(kr_ref[...], h))
        turned = pltpu.roll(flip(grad_scores), 0, 1, stride=1, stride_axis=0).astype(BF16)
        grad_place = grad_place + mm(turned, of_head(pk_ref[...], h))
        grad_p = grad_p + mm_tn(of_head(qp_flip, h), turned)
    grad_v = grad_v.astype(BF16)
    grad_k = (grad_k * SCALE).astype(BF16)
    grad_p = (grad_p * SCALE).astype(BF16)
    grad_c = grad_c * SCALE
    grad_place = grad_place * SCALE
    high = grad_place.astype(BF16)
    rest = (grad_place - high.astype(F32)).astype(BF16)
    grad_q = (grad_c + flip(high) + flip(rest)).astype(BF16)
    gq_ref[...] = grad_q
    both_ref[0:SLOT, :] = grad_k
    both_ref[SLOT:, :] = grad_v
    pay_ref[0:SLOT, :] = mm_tn(grad_q, normed).astype(BF16)
    pay_ref[SLOT : 3 * SLOT, :] = mm(both_ref[...], keys_in).astype(BF16)
    pay_ref[3 * SLOT : 4 * SLOT, :] = mm(grad_p, table_ref[...]).astype(BF16)
    biases = jnp.concatenate(
        [
            jnp.sum(grad_c, axis=0, keepdims=True),
            jnp.sum(grad_place, axis=0, keepdims=True),
            jnp.zeros((1, D - 2 * SLOT), F32),
        ],
        axis=1,
    )
    pay_ref[4 * SLOT :, :] = jnp.concatenate([biases, jnp.zeros((15, D), F32)], axis=0).astype(
        BF16
    )


def input_kernel(
    place_ref, x_ref, m0, m1, m2, m3, gm_ref, g_ref, both_0, both_1, both_2, both_3,
    gq_0, gq_1, gq_2, gq_3, h0, h1, h2, h3,
    grad_ref, vectors_ref,
    total_ref,
):
    me = place_ref[0]
    packs = (h0, h1, h2, h3)
    total = jnp.zeros((KEYS, D), F32)
    for both, pack in zip((both_0, both_1, both_2, both_3), packs):
        total = total + mm_tt(both[...], key_value_of(pack))
    total_ref[...] = total
    grad = total_ref[MEM:, :]
    for gq, pack in zip((gq_0, gq_1, gq_2, gq_3), packs):
        grad = grad + mm_nt(gq[...], query_of(pack))
    xhat, inverse = norm_parts(x_ref[...].astype(F32))
    grad_ref[...] = gm_ref[...] + norm_back(grad, g_ref[...], xhat, inverse)
    gain_grad = jnp.sum(grad * xhat, axis=0, keepdims=True)
    bias_grad = jnp.sum(grad, axis=0, keepdims=True) + jnp.sum(
        total_ref[:MEM, :], axis=0, keepdims=True
    )
    for k, block in enumerate((m0, m1, m2, m3)):
        seen, _ = norm_parts(block[...].astype(F32))
        start = pl.multiple_of((me ^ k) * SLOT, SLOT)
        gain_grad = gain_grad + jnp.sum(
            total_ref[pl.ds(start, SLOT), :] * seen, axis=0, keepdims=True
        )
    vectors_ref[...] = jnp.concatenate([gain_grad, bias_grad, jnp.zeros((6, D), F32)], axis=0)


def swap_with(values, axis, k):
    n = lax.axis_size(axis)
    return lax.ppermute(values, axis, [(i, i ^ k) for i in range(n)])


def turn(values, axis):
    return lax.all_to_all(values, axis, split_axis=0, concat_axis=0, tiled=True)


def by_steps():
    return lax.axis_size("dp") == 8


def when(values, after):
    return lax.optimization_barrier((values, after))[0]


def wide(*terms):
    return sum(t.astype(F32) for t in terms)


def part_of(values, index, count):
    size = values.shape[0] // count
    return lax.dynamic_slice_in_dim(values, index * size, size)


def in_order(place_ref, own, other, half):
    first = place_ref[1] == 0
    top = jnp.where(first, own[:half, :], other[:half, :])
    bottom = jnp.where(first, other[:half, :], own[:half, :])
    vectors = None
    if own.shape[0] > half:
        vectors = own[half:, :].astype(F32) + other[half:, :].astype(F32)
    return top, bottom, vectors


def outer_out_kernel(place_ref, own, other, out_ref):
    top, bottom, _ = in_order(place_ref, own, other, D // 2)
    out_ref[...] = jnp.concatenate([top, bottom], axis=0).T.astype(F32)


def inner_out_kernel(place_ref, own, other, inner_ref, output_ref, *rows_refs):
    half = (D + SLOT) // 2
    top, bottom, vectors = in_order(place_ref, own, other, half)
    inner_ref[0:half, :] = top.astype(F32)
    inner_ref[half:, :] = bottom[: D - half].astype(F32)
    output_ref[...] = bottom[D - half :].astype(F32)
    for n, ref in enumerate(rows_refs):
        ref[...] = vectors[n : n + 1]


def head_out_kernel(place_ref, own, other, q_ref, k_ref, v_ref, p_ref, *rows_refs):
    top, bottom, vectors = in_order(place_ref, own, other, D // 2)
    full = jnp.concatenate([top, bottom], axis=0)
    for n, ref in enumerate((q_ref, k_ref, v_ref, p_ref)):
        ref[...] = full[n * SLOT : (n + 1) * SLOT].T.astype(F32)
    content, place, gain, bias = rows_refs
    content[...] = vectors[0:1, :SLOT]
    place[...] = vectors[0:1, SLOT : 2 * SLOT]
    gain[...] = vectors[1:2]
    bias[...] = vectors[2:3]


class Summed:
    def __init__(self, place, rows, tail):
        self.place, self.rows, self.tail = place, rows, tail
        self.level = 0
        self.vectors = None

    def send_half(self, terms):
        bit = self.place[1 + self.level]
        self.kept = [part_of(t, bit, 2) for t in terms]
        sent = wide(*(part_of(t, 1 - bit, 2) for t in terms)).astype(BF16)
        self.got = swap_with(sent, "dp", 2**self.level)
        self.level += 1
        return sent

    def first(self, terms, after):
        terms = when(terms, after)
        if self.tail:
            self.vectors = wide(*(t[self.rows :] for t in terms)).astype(BF16)
        return self.send_half([t[: self.rows] for t in terms])

    def down(self, after):
        return self.send_half([*self.kept, when(self.got, after)])

    def send_back(self, part):
        self.level -= 1
        self.part = part
        message = part if self.vectors is None else jnp.concatenate([part, self.vectors], axis=0)
        self.got = swap_with(message, "dp", 2**self.level)
        return message

    def turn(self, after, vec=()):
        part = wide(*self.kept, when(self.got, after)).astype(BF16)
        if vec:
            lines = wide(*vec)[0:2].astype(BF16)
            self.vectors = jnp.concatenate([self.vectors[0:1], lines, self.vectors[3:]], axis=0)
        return self.send_back(part)

    def cross(self, after):
        part = wide(*self.kept, when(self.got, after)).astype(BF16)
        rows = part.shape[0] // 2
        self.kept, self.got = part[:rows], swap_with(part[rows:], "mp", 2)
        return part

    def turn_near(self, after):
        return self.send_back(wide(self.kept, when(self.got, after)).astype(BF16))

    def joined(self, got):
        rows = self.part.shape[0]
        low = self.place[1 + self.level] == 0
        other = got[:rows]
        if self.vectors is not None:
            self.vectors = wide(self.vectors, got[rows:]).astype(BF16)
        return jnp.concatenate(
            [jnp.where(low, self.part, other), jnp.where(low, other, self.part)], axis=0
        )

    def up(self, after):
        return self.send_back(self.joined(when(self.got, after)))

    def out(self, kernel, outs, after):
        own = self.part
        if self.vectors is not None:
            own = jnp.concatenate([own, self.vectors], axis=0)
        return call(kernel, outs, [self.place, own, self.got], smem=1, after=after, vmem=16)


def dp_sum(values):
    n = lax.axis_size("dp")
    rows = values.shape[0]
    got = turn(values.reshape(n, rows // n, D), "dp")
    part = jnp.sum(got.astype(F32), axis=0).astype(BF16)
    return turn(jnp.broadcast_to(part[None], (n,) + part.shape), "dp").reshape(rows, D)


def dp_vectors(values):
    n = lax.axis_size("dp")
    return jnp.sum(turn(jnp.broadcast_to(values[None], (n,) + values.shape), "dp"), axis=0)


def all_shards(values):
    one = swap_with(values, "mp", 1)
    two = swap_with(values, "mp", 2)
    three = swap_with(two, "mp", 1)
    return [values, one, two, three]


def local(
    block_input,
    memory,
    cotangent,
    neighbour_table,
    requests,
    counts,
    neighbour_slots,
    memory_lengths,
    document_lengths,
    first_gain,
    first_bias,
    query_weight,
    key_weight,
    value_weight,
    position_weight,
    content_bias,
    position_bias,
    output_weight,
    second_gain,
    second_bias,
    inner_weight,
    inner_bias,
    outer_weight,
    outer_bias,
    gate_weight,
):
    data_index = lax.axis_index("dp").astype(jnp.int32)
    place = jnp.stack(
        [lax.axis_index("mp").astype(jnp.int32)] + [data_index // 2**n % 2 for n in range(3)]
    )
    data_size = lax.axis_size("dp")
    capacity = requests.shape[1]
    row = lambda v: v.reshape(1, -1)
    g1, b1, g2, b2 = row(first_gain), row(first_bias), row(second_gain), row(second_bias)
    low_square = shape((SEG, D), BF16)
    block = shape((SLOT, D), BF16)

    wanted = turn(requests, "dp").reshape(requests.shape)

    *mem_own, head_pack = call(
        start_kernel,
        (block, block, block, block, shape((HEAD_PACK, D), BF16)),
        [
            place, memory, query_weight, key_weight, value_weight, position_weight,
            row(inner_bias), row(content_bias), row(position_bias),
        ],
        smem=1,
    )
    mem = [mem_own[0]] + [swap_with(mem_own[k], "mp", k) for k in (1, 2, 3)]
    heads = all_shards(head_pack)
    found = jnp.take(neighbour_table, wanted, axis=0, mode="clip")
    fetched = turn(found, "dp").reshape(data_size * capacity, D)
    (feed_pack,) = call(
        feed_pack_kernel,
        (shape((FEED_PACK, D), BF16),),
        [inner_weight, outer_weight, output_weight],
        vmem=56,
        after=[found],
    )
    feeds = all_shards(feed_pack)[:3]
    table = position_table()

    slot = lambda rows: shape((rows, SLOT), BF16)
    line = shape((1, D), F32)
    of_slot = (
        shape((2, SEG, KEYS), BF16),
        slot(SEG), slot(SEG), slot(KEYS), slot(KEYS), slot(KEYS), slot(SEG),
    )
    *results_a, keys_in = call(
        first_attend_kernel,
        of_slot * 2 + (line,) * 2 + (shape((KEYS, D), BF16),),
        [
            place, memory_lengths, document_lengths, *mem, block_input, g1, b1, table, *heads[:2],
        ],
        scratch=[pltpu.VMEM((SEG, KEYS), F32)],
        smem=3,
        after=[feed_pack],
        us=20,
        late=range(10, 13),
        early=(*range(14), 16),
    )
    results_b = call(
        attend_kernel,
        of_slot * 2 + (line,) * 2,
        [place, memory_lengths, document_lengths, keys_in, table, *heads[2:]],
        scratch=[pltpu.VMEM((SEG, KEYS), F32)],
        smem=3,
        us=20,
        early=range(14),
    )
    feeds.append(swap_with(when(feeds[2], results_b[0]), "mp", 1))
    saved = [r[7 * n : 7 * n + 7] for r in (results_a, results_b) for n in range(2)]
    inner_biases = [*results_a[14:16], *results_b[14:16]]
    attended = [v[-1] for v in saved]

    square = shape((SEG, D), F32)
    units = shape((4, SEG, D), BF16)
    middle, hidden, normed_middle, activation, slope = call(
        feed_kernel,
        (square, square, low_square, units, units),
        [block_input, *attended, g2, b2, *inner_biases, *feeds, row(outer_bias)],
        us=10,
        early=(0, 2, 3, 4),
    )

    pair = shape((2, D, D), BF16)
    slot_grad = shape((SEG, SLOT), BF16)
    inner_pair = shape((2, FEED_ROWS, D), BF16)
    mixed, outer_keep, outer_send, grad_middle, *grad_att, inner_keep, inner_send = call(
        mix_kernel,
        (low_square, pair, pair, square, *[slot_grad] * 4, inner_pair, inner_pair),
        [
            place, document_lengths, fetched, neighbour_slots, cotangent, hidden,
            row(gate_weight), g2, middle, normed_middle, activation, slope, *attended, *feeds,
        ],
        scratch=[pltpu.VMEM((SEG, D), F32), pltpu.VMEM((4, SEG, D), BF16)],
        smem=2,
        us=20,
        vmem=56,
        late=range(8, 20),
        early=(0, 1, 2),
    )

    def attend_back(n, after):
        return call(
            attend_back_kernel,
            (shape((HEAD_ROWS, D), BF16), shape((2 * SLOT, KEYS), BF16), shape((SEG, SLOT), BF16)),
            [keys_in, table, *saved[n][:-1], grad_att[n]],
            us=9,
            after=after,
            vmem=20,
        )

    def two(keep, send, after):
        keep, got = when((keep, swap_with(send, "mp", 1)), after)
        near, far = (wide(keep[n], got[n]).astype(BF16) for n in range(2))
        return near, swap_with(far, "mp", 2)

    steps = by_steps()
    outer = Summed(place, 2 * D, 0)
    keep, got = when((outer_keep, swap_with(outer_send, "mp", 1)), grad_middle)
    if steps:
        both = wide(keep, got).reshape(2, 8, D // 8, D).swapaxes(0, 1).reshape(2 * D, D).astype(BF16)
        at = outer.first([both], [grad_middle])
    else:
        at = outer_near = wide(keep[0], got[0]).astype(BF16)
        outer_far = swap_with(wide(keep[1], got[1]).astype(BF16), "mp", 2)
    pay_3, both_3, gq_3 = attend_back(3, [at])
    inner_near, inner_far = two(inner_keep, inner_send, [gq_3])
    pay_2, both_2, gq_2 = attend_back(2, [inner_near])
    head_far = wide(*when((pay_2, swap_with(pay_3, "mp", 1)), gq_2)).astype(BF16)
    head_got = swap_with(head_far, "mp", 2)
    inner, head = Summed(place, D + SLOT, 1), Summed(place, D, 1)
    eight = shape((8, D), F32)

    def input_back(after):
        return call(
            input_kernel,
            (square, eight),
            [
                place, block_input, *mem, grad_middle, g1, both_0, both_1, both_2, both_3,
                gq_0, gq_1, gq_2, gq_3, *heads,
            ],
            scratch=[pltpu.VMEM((KEYS, D), F32)],
            smem=1,
            after=after,
            us=6,
            vmem=20,
        )

    weight = shape((D, SLOT), F32)
    short = shape((1, SLOT), F32)
    head_outs = (weight,) * 4 + (short, short, line, line)
    inner_outs = (square, shape((SLOT, D), F32)) + (line,) * 5
    if steps:
        at = outer.down([head_far])
        pay_1, both_1, gq_1 = attend_back(1, [at])
        at = outer.down([gq_1])
        pay_0, both_0, gq_0 = attend_back(0, [at])
        at = inner.first([inner_near, inner_far], [gq_0])
        input_grad, vectors = input_back([at])
        at = outer.cross([vectors])
        at = head.first([pay_0, swap_with(pay_1, "mp", 1), head_got], [at])
        at = inner.down([at])
        at = outer.turn_near([at])
        at = head.down([at])
        at = inner.down([at])
        vectors = wide(*when((vectors, swap_with(vectors, "mp", 1)), at))
        at = outer.up([vectors])
        at = head.down([at])
        at = inner.turn([at])
        at = outer.up([at])
        at = head.turn([at], [vectors, swap_with(vectors, "mp", 2)])
        at = inner.up([at])
        at = head.up([at])
        (outer_grad,) = outer.out(outer_out_kernel, (square,), [at])
        at = inner.up([outer_grad])
        at = head.up([at])
        inner_grad, output_grad, *rows = inner.out(inner_out_kernel, inner_outs, [at])
        query_grad, key_grad, value_grad, place_grad, *head_rows = head.out(
            head_out_kernel, head_outs, [inner_grad]
        )
        content_grad, place_bias_grad, gain_grad, bias_grad = (v[0] for v in head_rows)
        rows = [v[0] for v in rows]
    else:
        pay_1, both_1, gq_1 = attend_back(1, [head_far])
        pay_0, both_0, gq_0 = attend_back(0, [gq_1])
        outer = wide(outer_near, outer_far)
        inner = wide(inner_near, inner_far)
        head = wide(pay_0, swap_with(pay_1, "mp", 1), head_got)
        input_grad, vectors = input_back([gq_0])
        vectors = vectors + swap_with(vectors, "mp", 1)
        vectors = dp_vectors(vectors + swap_with(vectors, "mp", 2))
        outer_grad = dp_sum(outer.astype(BF16)).astype(F32).T
        inner_grad = dp_sum(inner[: D + SLOT].astype(BF16)).astype(F32)
        rows = dp_vectors(inner[D + SLOT :])
        inner_grad, output_grad = inner_grad[:D], inner_grad[D:]
        head_rows = dp_vectors(head[4 * SLOT :])
        grads = dp_sum(head[: 4 * SLOT].astype(BF16)).astype(F32)
        query_grad, key_grad, value_grad, place_grad = (
            grads[n * SLOT : (n + 1) * SLOT].T for n in range(4)
        )
        content_grad, place_bias_grad = head_rows[0, :SLOT], head_rows[0, SLOT : 2 * SLOT]
        gain_grad, bias_grad = vectors[0], vectors[1]
    return (
        mixed,
        input_grad,
        gain_grad,
        bias_grad,
        query_grad,
        key_grad,
        value_grad,
        place_grad,
        content_grad,
        place_bias_grad,
        output_grad,
        rows[1],
        rows[2],
        inner_grad,
        rows[0],
        outer_grad,
        rows[3],
        rows[4],
    )


def solution(mesh):
    return jax.shard_map(
        local,
        mesh=mesh,
        in_specs=(
            P(("dp", "mp"), None),
            P("dp", "mp", None),
            P(("dp", "mp"), None),
            P("dp", None),
            P(("dp", "mp"), None),
            P(("dp", "mp")),
            P(("dp", "mp"), None),
            P("dp"),
            P("dp"),
            P(),
            P(),
            P(None, "mp"),
            P(None, "mp"),
            P(None, "mp"),
            P(None, "mp"),
            P("mp"),
            P("mp"),
            P("mp", None),
            P(),
            P(),
            P(None, "mp"),
            P("mp"),
            P("mp", None),
            P(),
            P(),
        ),
        out_specs=(
            P(("dp", "mp"), None),
            P(("dp", "mp"), None),
            P(),
            P(),
            P(None, "mp"),
            P(None, "mp"),
            P(None, "mp"),
            P(None, "mp"),
            P("mp"),
            P("mp"),
            P("mp", None),
            P(),
            P(),
            P(None, "mp"),
            P("mp"),
            P("mp", None),
            P(),
            P(),
        ),
        check_vma=False,
    )
```
